512 devices in a mesh: vocab: 128 (over x, z, core), batch: 4 (over y).
Axes of the slice: x: 4, y: 4, z: 16, core: 2. Of those that a mesh axis runs over, the one named last changes fastest.
Arguments:
- hidden: bfloat16 [4096, 1024], P(('vocab', 'batch'))
- embedding: bfloat16 [131072, 1024], P('vocab')
- block_counts: int32 [1024], P('vocab'), may hold values from 1 to 4095
- lang_blocks: int32 [200, 64], replicated, may hold values from -1 to 1023, as said below
- sent_lang: int32 [64], replicated, may hold values from 0 to 199
- targets: int32 [4096], replicated, may hold values from 0 to 131071, as said below
Outputs:
- token_loss: float32 [4096], P(('vocab', 'batch'))
- grad_embed: bfloat16 [131072, 1024], P(('vocab', 'batch'))
The draws below stay inside these ranges and needn't reach their ends.
Inputs may be any that keep to these rules, and one draw needn't show every extreme that they name: `lang_blocks`: each list holds distinct block numbers and then -1 padding; the first entry of every list is block 0; at least 16 entries are blocks, and some language fills all 64 entries. `targets`: the target of token t lies in a block listed for the language of sentence t // 64.
All inputs are finite; a program needn't handle non-finite values.
Results may differ from the reference program's by a relative error of at most 0.0075.
Values may be sent and summed in bfloat16 or wider, within the bound.
A program may use at most 64 MiB of HBM per device.

```python
import math
import jax
import jax.numpy as jnp
from jax import lax

D = 1024
BLOCK = 128
LANGS = 200
LB = 64
SEQ = 64
TOK_DEV = 8
NBLK = 1024
VOCAB = 131072
TOKENS = 4096
SENTS = 64
N_BATCH = 4


def first_block(key):
    spread = 3.0 / math.sqrt(D)
    return jax.random.truncated_normal(jax.random.fold_in(key, 401), -6.0, 6.0, (BLOCK, D), jnp.float32) * spread


def language_lists(key):
    base_key = jax.random.fold_in(key, 101)

    def one_language(language):
        shuffled = jax.random.permutation(jax.random.fold_in(base_key, language), NBLK - 1) + 1
        return shuffled[:LB - 1].astype(jnp.int32)
    chosen = jax.vmap(one_language)(jnp.arange(LANGS, dtype=jnp.int32))
    lists = jnp.concatenate([jnp.zeros((LANGS, 1), jnp.int32), chosen], axis=1)
    full_language = LANGS - 1
    full_rest = (jax.random.permutation(jax.random.fold_in(key, 105), NBLK - 2) + 1)[:LB - 2].astype(jnp.int32)
    full_row = jnp.concatenate([jnp.zeros((1,), jnp.int32), jnp.full((1,), NBLK - 1, jnp.int32), full_rest])
    lists = lists.at[full_language].set(full_row)
    counts = jax.random.randint(jax.random.fold_in(key, 102), (LANGS,), LB // 4, LB + 1)
    short_language = jax.random.randint(jax.random.fold_in(key, 104), (), 0, LANGS - 1)
    language_ids = jnp.arange(LANGS, dtype=jnp.int32)
    counts = jnp.where(language_ids == full_language, LB, counts)
    counts = jnp.where(language_ids == short_language, LB // 4, counts)
    padded = jnp.where(jnp.arange(LB, dtype=jnp.int32)[None, :] < counts[:, None], lists, -1)
    return (padded.astype(jnp.int32), counts.astype(jnp.int32))


def sentence_languages(key):
    drawn = jax.random.randint(jax.random.fold_in(key, 201), (SENTS,), 0, LANGS).astype(jnp.int32)
    drawn = drawn.at[0].set(0)
    return drawn.at[SENTS - 1].set(LANGS - 1).astype(jnp.int32)


def draw_lang_blocks(key, part):
    return language_lists(key)[0]


def draw_sent_lang(key, part):
    return sentence_languages(key)


def draw_targets(key, part):
    lists, counts = language_lists(key)
    languages = sentence_languages(key)
    token_language = jnp.repeat(languages, SEQ)
    position = jax.random.randint(jax.random.fold_in(key, 301), (TOKENS,), 0, LB) % counts[token_language]
    chosen_block = lists[token_language, position]
    within = jax.random.randint(jax.random.fold_in(key, 302), (TOKENS,), 0, BLOCK)
    drawn = (chosen_block * BLOCK + within).astype(jnp.int32)
    drawn = drawn.at[0].set(0)
    return drawn.at[TOKENS - 1].set(VOCAB - 1).astype(jnp.int32)


def draw_embedding(key, part):
    spread = 3.0 / math.sqrt(D)
    remainder = jax.random.truncated_normal(jax.random.fold_in(key, 402), -6.0, 6.0, (VOCAB - BLOCK, D), jnp.float32) * spread
    return jnp.concatenate([first_block(key), remainder], axis=0).astype(jnp.bfloat16)


def draw_hidden(key, part):
    return jax.random.truncated_normal(jax.random.fold_in(key, 502), -6.0, 6.0, (TOKENS, D), jnp.float32).astype(jnp.bfloat16)


def with_ends(values, rng, least, top_value):
    longest = values.shape.index(max(values.shape))
    spots = []
    for shift in (0, 1):
        where = [jax.random.randint(jax.random.fold_in(rng, axis), (), 0, length) for axis, length in enumerate(values.shape)]
        where[longest] = (where[longest] + shift) % values.shape[longest]
        spots.append(tuple(where))
    return values.at[spots[0]].set(least).at[spots[1]].set(top_value)


def setup_inputs(seed: int = 0) -> dict:
    seeds = jax.random.split(jax.random.key(seed), 7)
    return {
        "hidden": draw_hidden(jax.random.fold_in(seeds[6], 71), 0),
        "embedding": draw_embedding(jax.random.fold_in(seeds[6], 71), 0),
        "block_counts": with_ends(jax.random.randint(seeds[2], (NBLK,), 1, 4096), jax.random.fold_in(seeds[2], 1), 1, 4095).astype(jnp.int32),
        "lang_blocks": draw_lang_blocks(jax.random.fold_in(seeds[6], 71), 0),
        "sent_lang": draw_sent_lang(jax.random.fold_in(seeds[6], 71), 0),
        "targets": draw_targets(jax.random.fold_in(seeds[6], 71), 0),
    }


def sentence_terms(hidden, embedding, log_sampling, lang_blocks, sent_lang, targets, sentence_index):
    blocks = lang_blocks[sent_lang[sentence_index]]
    usable = blocks >= 0
    safe_blocks = jnp.where(usable, blocks, 0).astype(jnp.int32)
    row_ids = (safe_blocks[:, None] * BLOCK + jnp.arange(BLOCK, dtype=jnp.int32)[None, :]).reshape(-1)
    candidates = jnp.take(embedding, row_ids, axis=0)
    first_token = (sentence_index * SEQ).astype(jnp.int32)
    hidden_rows = lax.dynamic_slice_in_dim(hidden, first_token, SEQ, 0)
    target_ids = lax.dynamic_slice_in_dim(targets, first_token, SEQ, 0)
    raw_scores = lax.dot_general(hidden_rows, candidates, (((1,), (1,)), ((), ())), preferred_element_type=jnp.float32)
    logits = raw_scores.reshape(SEQ, LB, BLOCK) - log_sampling[safe_blocks][None, :, None]
    allowed = usable[None, :, None]
    peak_value = jnp.max(jnp.where(allowed, logits, -jnp.inf), axis=(1, 2))
    denominator = jnp.sum(jnp.where(allowed, jnp.exp(logits - peak_value[:, None, None]), 0.0), axis=(1, 2))
    log_total = peak_value + jnp.log(denominator)
    is_target = (row_ids.reshape(LB, BLOCK)[None, :, :] == target_ids[:, None, None]) & allowed
    target_logit = jnp.sum(jnp.where(is_target, logits, 0.0), axis=(1, 2))
    loss_part = log_total - target_logit
    softmax_weights = jnp.where(allowed, jnp.exp(logits - log_total[:, None, None]), 0.0)
    grad_logits = (softmax_weights - is_target.astype(jnp.float32)).astype(jnp.bfloat16).reshape(SEQ, LB * BLOCK)
    token_group = ((jnp.arange(SEQ, dtype=jnp.int32) + first_token) // TOK_DEV) % N_BATCH
    return loss_part, grad_logits, row_ids, usable, hidden_rows, token_group


def reference(hidden, embedding, block_counts, lang_blocks, sent_lang, targets):
    log_sampling = jnp.log(block_counts.astype(jnp.float32))
    sentence_list = jnp.arange(SENTS, dtype=jnp.int32)

    def loss_only(sentence_index):
        return sentence_terms(hidden, embedding, log_sampling, lang_blocks, sent_lang, targets, sentence_index)[0]

    token_loss = lax.map(loss_only, sentence_list).reshape(-1)
    summed = jnp.zeros((VOCAB, D), jnp.float32)
    for source in range(N_BATCH):
        def add_sentence(accumulated, sentence_index):
            loss_part, grad_logits, row_ids, usable, hidden_rows, token_group = sentence_terms(
                hidden, embedding, log_sampling, lang_blocks, sent_lang, targets, sentence_index)
            keep = token_group == source
            weighted = jnp.where(keep[:, None], grad_logits, jnp.zeros_like(grad_logits))
            contribution = lax.dot_general(weighted, hidden_rows, (((0,), (0,)), ((), ())), preferred_element_type=jnp.float32)
            contribution = contribution * jnp.repeat(usable, BLOCK)[:, None].astype(jnp.float32)
            return accumulated.at[row_ids].add(contribution), None

        accumulated, ignored = lax.scan(add_sentence, jnp.zeros((VOCAB, D), jnp.float32), sentence_list)
        rounded = lax.optimization_barrier(accumulated.astype(jnp.bfloat16))
        summed = summed + rounded.astype(jnp.float32)
    return token_loss, summed.astype(jnp.bfloat16)
```

```python
import functools

import jax
import jax.numpy as jnp
from jax import lax
from jax.experimental import pallas as pl
from jax.experimental.pallas import tpu as pltpu
from jax.sharding import PartitionSpec as P

MESH = pl.DeviceIdType.MESH
F32, BF16 = jnp.float32, jnp.bfloat16
NX, NZ, NY = 4, 16, 4
D = 1024
HALF = 512
ROWS = 1024
TOK = 1024
NB = 8
BLK = 128
QROWS = 256
CHUNK = 256
FILL = -3e38
REACH = 4
ZORDER = [0] + [s * k for k in range(1, 8) for s in (1, -1)] + [-8]
XPEERS = (1, 3, 2)


def remote(src, dst, send, recv, device):
    return pltpu.make_async_remote_copy(
        src_ref=src, dst_ref=dst, send_sem=send, recv_sem=recv,
        device_id=device, device_id_type=MESH,
    )


def merge(parts):
    top = functools.reduce(jnp.maximum, parts)
    total = functools.reduce(jnp.add, [jnp.exp(p - top) for p in parts])
    return top + jnp.log(total)


def kernel(
    hid_ref, emb_ref, counts_ref, lists_ref, lane_ref,
    loss_ref, grad_ref,
    table, tokens, logits, probs, swap, allowed, peak_row, total_row,
    s1, s2, t1, t2, lse_out, l1_out, tgt_out, tsum_out, send_buf, recv_buf, out_buf,
    sem_table, sem_swap, sem_z_send, sem_z, sem_x_send, sem_x, sem_c_send, sem_c,
    sem_s1s, sem_s1, sem_s2s, sem_s2, sem_t1s, sem_t1, sem_t2s, sem_t2, sem_rs, sem_rr,
    sem_out,
):
    v, y = lax.axis_index("vocab"), lax.axis_index("batch")
    c = lax.rem(v, 2)
    z = lax.rem(lax.div(v, 2), NZ)
    x = lax.div(v, 2 * NZ)

    def dev(px, pz, pc, py):
        return {"vocab": (px * NZ + pz) * 2 + pc, "batch": py}

    def at_z(k):
        return dev(x, lax.rem(z + k + 2 * NZ, NZ), c, y)

    def at_x(k, flip=0):
        return dev(lax.rem(x + k, NX), z, (1 - c) if flip else c, y)

    partner = dev(x, z, 1 - c, y)
    xc_peers = [(k, f) for f in (0, 1) for k in range(NX) if (k, f) != (0, 0)]

    load = pltpu.make_async_copy(emb_ref, table, sem_table)
    load.start()

    barrier = pltpu.get_barrier_semaphore()
    near = [at_x(k, f) for k, f in xc_peers]
    near += [at_z(s * k) for k in range(1, REACH + 1) for s in (1, -1)]
    near += [dev(x, z, c, lax.rem(y + k, NY)) for k in range(1, NY)]
    for peer in near:
        pl.semaphore_signal(barrier, inc=1, device_id=peer, device_id_type=MESH)
    pl.semaphore_wait(barrier, len(near))

    mine = hid_ref[...].astype(F32)
    low, high = mine[:, :HALF], mine[:, HALF:]
    swap[0] = jnp.where(c == 0, high, low)
    trade = remote(swap.at[0], swap.at[1], sem_swap.at[0], sem_swap.at[1], partner)
    trade.start()

    lists = lists_ref[...]
    columns = [
        jnp.any(lists == v * NB + b, axis=1, keepdims=True).astype(F32) for b in range(NB)
    ]
    member = jnp.concatenate(columns, axis=1)
    langs = lists.shape[0]
    hit = (lax.broadcasted_iota(jnp.int32, (langs, TOK), 0) == lane_ref[0:1, :]).astype(F32)
    allowed[...] = lax.dot_general(
        member, hit, (((0,), (0,)), ((), ())), preferred_element_type=F32
    )

    trade.wait_recv()
    kept = jnp.where(c == 0, low, high)
    first = jnp.where(c == 0, kept, swap[1])
    second = jnp.where(c == 0, swap[1], kept)

    def spot(px, pz, n=16):
        row = pl.multiple_of((px * NZ + pz) * 16, 16)
        return tokens.at[pl.ds(row, n), pl.ds(pl.multiple_of(c * HALF, HALF), HALF)]

    own_row = pl.multiple_of((x * NZ + z) * 16, 16)
    tokens[pl.ds(own_row, 16), pl.ds(pl.multiple_of(c * HALF, HALF), HALF)] = (
        jnp.concatenate([first, second], axis=0).astype(BF16)
    )

    def z_send(origin, step):
        block = spot(x, lax.rem(z + origin + 2 * NZ, NZ))
        remote(block, block, sem_z_send, sem_z.at[origin - step + NZ], at_z(step)).start()

    def x_wait(j, k):
        block = spot(lax.rem(x + XPEERS[j], NX), lax.rem(z + k + 2 * NZ, NZ))
        remote(block, block, sem_x_send.at[j], sem_x.at[j, k + NZ], partner).wait_recv()
        remote(block, block, sem_c_send.at[j], sem_c.at[j], partner).start()

    for k in range(1, REACH + 1):
        z_send(0, k)
        z_send(0, -k)
    lag = 4
    for n, k in enumerate(ZORDER):
        block = spot(x, lax.rem(z + k + 2 * NZ, NZ))
        if k:
            remote(block, block, sem_z_send, sem_z.at[k + NZ], partner).wait_recv()
        if k == -REACH:
            for step in range(1, NZ // 2 - REACH + 1):
                z_send(k, step)
        if k == REACH:
            for step in range(1, NZ // 2 - REACH):
                z_send(k, -step)
        for j, xk in enumerate(XPEERS):
            seen = XPEERS.index(NX - xk)
            remote(
                block, block, sem_x_send.at[j], sem_x.at[seen, k + NZ], at_x(xk)
            ).start()
        remote(block, block, sem_c_send.at[3], sem_c.at[3], partner).start()
        if n >= lag:
            for j in range(3):
                x_wait(j, ZORDER[n - lag])
    for k in ZORDER[NZ - lag:]:
        for j in range(3):
            x_wait(j, k)

    load.wait()
    log_counts = jnp.log(counts_ref[...].astype(F32))
    word = v * ROWS + lax.broadcasted_iota(jnp.int32, (BLK, CHUNK), 0)

    for j, xk in ((3, 0), (0, XPEERS[0]), (1, XPEERS[1]), (2, XPEERS[2])):
        px = lax.rem(x + xk, NX)
        whole = spot(px, 0, CHUNK)
        remote(whole, whole, sem_c_send.at[j], sem_c.at[j], partner).wait_recv()
        lane = pl.multiple_of(px * CHUNK, CHUNK)
        held = tokens[pl.ds(lane, CHUNK), :]
        target = lane_ref[1:2, pl.ds(lane, CHUNK)]
        top = jnp.full((1, CHUNK), FILL, F32)
        hit_logit = jnp.zeros((1, CHUNK), F32)
        for b in range(NB):
            score = lax.dot_general(
                table[b * BLK:(b + 1) * BLK, :], held, (((1,), (1,)), ((), ())),
                preferred_element_type=F32,
            ) - log_counts[0:1, b:b + 1]
            score = jnp.where(allowed[b:b + 1, pl.ds(lane, CHUNK)] > 0.5, score, FILL)
            logits[b * BLK:(b + 1) * BLK, pl.ds(lane, CHUNK)] = score
            top = jnp.maximum(top, jnp.max(score, axis=0, keepdims=True))
            hit_logit += jnp.sum(
                jnp.where(word + b * BLK == target, score, 0.0), axis=0, keepdims=True
            )
        total = jnp.zeros((1, CHUNK), F32)
        for b in range(NB):
            share = jnp.exp(logits[b * BLK:(b + 1) * BLK, pl.ds(lane, CHUNK)] - top)
            logits[b * BLK:(b + 1) * BLK, pl.ds(lane, CHUNK)] = share
            total += jnp.sum(share, axis=0, keepdims=True)
        peak_row[0:1, pl.ds(lane, CHUNK)] = top
        local = top + jnp.log(total)
        for r in range(CHUNK // 128):
            row = px * (CHUNK // 128) + r
            lse_out[row] = local[:, r * 128:(r + 1) * 128]
            tgt_out[row] = hit_logit[:, r * 128:(r + 1) * 128]

    slot = x * 2 + c
    for i, (k, f) in enumerate(xc_peers):
        remote(lse_out, s1.at[slot], sem_s1s.at[i], sem_s1.at[slot], at_x(k, f)).start()

    def slot_of(k, f):
        return lax.rem(x + k, NX) * 2 + ((1 - c) if f else c)

    parts = [lse_out[...]]
    for i, (k, f) in enumerate(xc_peers):
        there = slot_of(k, f)
        remote(lse_out, s1.at[there], sem_s1s.at[i], sem_s1.at[there], partner).wait_recv()
        parts.append(s1[there])
    l1 = merge(parts)
    l1_out[...] = l1
    z_far_first = sorted(range(1, NZ), key=lambda k: -min(k, NZ - k))
    for k in z_far_first:
        remote(l1_out, s2.at[z], sem_s2s.at[k], sem_s2.at[z], at_z(k)).start()
    for i, (k, f) in enumerate(xc_peers):
        remote(tgt_out, t1.at[slot], sem_t1s.at[i], sem_t1.at[slot], at_x(k, f)).start()
    tsum = tgt_out[...]
    for i, (k, f) in enumerate(xc_peers):
        there = slot_of(k, f)
        remote(tgt_out, t1.at[there], sem_t1s.at[i], sem_t1.at[there], partner).wait_recv()
        tsum = tsum + t1[there]
    tsum_out[...] = tsum
    for k in range(1, NZ):
        far = lax.rem(z + k, NZ)
        row = x * 2 + lax.div(far, 8)
        remote(
            tsum_out.at[row], t2.at[z], sem_t2s.at[k], sem_t2.at[z], at_z(k)
        ).start()

    parts = [l1]
    for k in range(1, NZ):
        there = lax.rem(z + k, NZ)
        remote(l1_out, s2.at[there], sem_s2s.at[k], sem_s2.at[there], partner).wait_recv()
        parts.append(s2[there])
    log_total = merge(parts)
    l1_out_row = x * 2 + lax.div(z, 8)
    for r in range(TOK // 128):
        total_row[0:1, r * 128:(r + 1) * 128] = log_total[r]

    scale = jnp.exp(peak_row[0:1, :] - total_row[0:1, :])
    word = v * ROWS + lax.broadcasted_iota(jnp.int32, (QROWS, TOK), 0)

    def quarter(q):
        row = pl.multiple_of(q * QROWS, QROWS)
        weights = logits[pl.ds(row, QROWS), :] * scale
        weights = weights - (word + row == lane_ref[1:2, :]).astype(F32)
        probs[...] = weights.astype(BF16)
        return lax.dot_general(
            probs[...], tokens[...], (((1,), (0,)), ((), ())), preferred_element_type=F32
        )

    for i, k in enumerate((2, 1, 3)):
        py = lax.rem(y + k, NY)
        send_buf[i] = quarter(py).astype(BF16)
        seen = (2, 1, 3).index(NY - k)
        remote(
            send_buf.at[i], recv_buf.at[seen], sem_rs.at[i], sem_rr.at[seen],
            dev(x, z, c, py),
        ).start()
    own = quarter(y)

    tgt = tsum_out[l1_out_row]
    for k in range(1, NZ):
        there = lax.rem(z + k, NZ)
        remote(
            tsum_out.at[0], t2.at[there], sem_t2s.at[k], sem_t2.at[there], partner
        ).wait_recv()
        tgt = tgt + t2[there]
    lane0 = lax.rem(z, 8) * 16 + c * 8
    lse_row = total_row[0:1, pl.ds(pl.multiple_of(l1_out_row * 128, 128), 128)]
    loss = jnp.broadcast_to(lse_row - tgt, (8, 128))
    loss_ref[...] = pltpu.roll(loss, lax.rem(128 - lane0, 128), 1)

    for i in (1, 2, 0):
        remote(
            send_buf.at[i], recv_buf.at[i], sem_rs.at[i], sem_rr.at[i], partner
        ).wait_recv()
        own = own + recv_buf[i].astype(F32)
    out_buf[...] = own.astype(BF16)
    put = pltpu.make_async_copy(out_buf, grad_ref, sem_out)
    put.start()

    trade.wait_send()
    remote(
        tokens.at[pl.ds(0, 240), pl.ds(0, HALF)], tokens.at[pl.ds(0, 240), pl.ds(0, HALF)],
        sem_z_send, sem_z.at[0], partner,
    ).wait_send()
    whole = tokens.at[pl.ds(0, CHUNK), pl.ds(0, HALF)]
    for j in range(3):
        remote(whole, whole, sem_x_send.at[j], sem_x.at[j, 0], partner).wait_send()
    for j in range(4):
        remote(whole, whole, sem_c_send.at[j], sem_c.at[j], partner).wait_send()
    for i in range(7):
        remote(lse_out, s1.at[0], sem_s1s.at[i], sem_s1.at[0], partner).wait_send()
        remote(tgt_out, t1.at[0], sem_t1s.at[i], sem_t1.at[0], partner).wait_send()
    for k in range(1, NZ):
        remote(l1_out, s2.at[0], sem_s2s.at[k], sem_s2.at[0], partner).wait_send()
        remote(tsum_out.at[0], t2.at[0], sem_t2s.at[k], sem_t2.at[0], partner).wait_send()
    for i in range(3):
        remote(send_buf.at[i], recv_buf.at[i], sem_rs.at[i], sem_rr.at[i], partner).wait_send()
    put.wait()


def body(hidden, embedding, block_counts, lang_blocks, sent_lang, targets):
    v, y = lax.axis_index("vocab"), lax.axis_index("batch")
    lang_lane = jnp.broadcast_to(sent_lang[:, None], (64, 16)).reshape(1, TOK)
    plane = lax.dynamic_index_in_dim(targets.reshape(128, NY, 8), y, 1, keepdims=False)
    lanes = jnp.concatenate(
        [lang_lane, plane.reshape(1, TOK), jnp.zeros((6, TOK), jnp.int32)], axis=0
    )
    vmem, dma = pltpu.VMEM, pltpu.SemaphoreType.DMA
    spec = pl.BlockSpec(memory_space=pltpu.VMEM)
    loss, grad = pl.pallas_call(
        kernel,
        out_shape=(
            jax.ShapeDtypeStruct((8, 128), F32),
            jax.ShapeDtypeStruct((QROWS, D), BF16),
        ),
        in_specs=[spec, pl.BlockSpec(memory_space=pl.ANY), spec, spec, spec],
        out_specs=(spec, pl.BlockSpec(memory_space=pl.ANY)),
        scratch_shapes=[
            vmem((ROWS, D), BF16),
            vmem((TOK, D), BF16),
            vmem((ROWS, TOK), F32),
            vmem((QROWS, TOK), BF16),
            vmem((2, 8, HALF), F32),
            vmem((NB, TOK), F32),
            vmem((8, TOK), F32),
            vmem((8, TOK), F32),
            vmem((8, 8, 1, 128), F32),
            vmem((NZ, 8, 1, 128), F32),
            vmem((8, 8, 1, 128), F32),
            vmem((NZ, 1, 128), F32),
            vmem((8, 1, 128), F32),
            vmem((8, 1, 128), F32),
            vmem((8, 1, 128), F32),
            vmem((8, 1, 128), F32),
            vmem((3, QROWS, D), BF16),
            vmem((3, QROWS, D), BF16),
            vmem((QROWS, D), BF16),
            dma, dma((2,)), dma, dma((2 * NZ,)), dma((3,)), dma((3, 2 * NZ)),
            dma((4,)), dma((4,)), dma((7,)), dma((8,)), dma((NZ,)), dma((NZ,)),
            dma((7,)), dma((8,)), dma((NZ,)), dma((NZ,)), dma((3,)), dma((3,)), dma,
        ],
        compiler_params=pltpu.CompilerParams(
            collective_id=0, has_side_effects=True, vmem_limit_bytes=48 << 20
        ),
    )(hidden, embedding, block_counts.reshape(1, NB), lang_blocks, lanes)
    return loss[0, :8], grad


def solution(mesh):
    in_specs = (P(("vocab", "batch"), None), P("vocab", None), P("vocab"), P(), P(), P())
    out_specs = (P(("vocab", "batch")), P(("vocab", "batch"), None))
    return jax.shard_map(body, mesh=mesh, in_specs=in_specs, out_specs=out_specs, check_vma=False)
```

```python
import functools

import jax
import jax.numpy as jnp
from jax import lax
from jax.experimental import pallas as pl
from jax.experimental.pallas import tpu as pltpu
from jax.sharding import PartitionSpec as P

MESH = pl.DeviceIdType.MESH
F32, BF16, I32 = jnp.float32, jnp.bfloat16, jnp.int32
NX, NZ, NY = 4, 16, 4
D = 1024
HALF = 512
ROWS = 1024
TOK = 1024
NB = 8
BLK = 128
QROWS = 256
CHUNK = 256
FILL = -3e38
REACH = 4
ZORDER = [0] + [s * k for k in range(1, 8) for s in (1, -1)] + [-8]
XPEERS = (1, 3, 2)
XC_PEERS = [(k, f) for f in (0, 1) for k in range(NX) if (k, f) != (0, 0)]
CHUNKS = (0, 3, 1, 2)


def remote(src, dst, send, recv, device):
    return pltpu.make_async_remote_copy(
        src_ref=src, dst_ref=dst, send_sem=send, recv_sem=recv,
        device_id=device, device_id_type=MESH,
    )


def merge(parts):
    top = functools.reduce(jnp.maximum, parts)
    total = functools.reduce(jnp.add, [jnp.exp(p - top) for p in parts])
    return top + jnp.log(total)


def dot(a, b, contract):
    return lax.dot_general(a, b, (contract, ((), ())), preferred_element_type=F32)


def kernel(
    hid_hbm, emb_hbm, counts_hbm, lists_hbm, sent_hbm, targets_hbm,
    loss_ref, grad_ref,
    hid, table, counts, lists, sent, targets,
    tokens, tokens2, logits, logits2, probs, sums, swap, allowed, rows,
    s1, s2, t1, t2, lse_out, l1_out, tgt_out, tsum_out, l_out, l_in,
    send_buf, recv_buf, out_buf,
    sem_load, sem_swap, sem_z_send, sem_z, sem_x_send, sem_x, sem_c_send, sem_c,
    sem_y_send, sem_y, sem_c2_send, sem_c2,
    sem_s1s, sem_s1, sem_s2s, sem_s2, sem_t1s, sem_t1, sem_t2s, sem_t2,
    sem_l, sem_rs, sem_rr, sem_out,
):
    v, y = lax.axis_index("vocab"), lax.axis_index("batch")
    c = lax.rem(v, 2)
    z = lax.rem(lax.div(v, 2), NZ)
    x = lax.div(v, 2 * NZ)

    def dev(px, pz, pc, py):
        return {"vocab": (px * NZ + pz) * 2 + pc, "batch": py}

    def at_z(k):
        return dev(x, lax.rem(z + k + 2 * NZ, NZ), c, y)

    def at_x(k, flip=0):
        return dev(lax.rem(x + k, NX), z, (1 - c) if flip else c, y)

    def at_y(k):
        return dev(x, z, c, lax.rem(y + k, NY))

    partner = dev(x, z, 1 - c, y)
    across = at_y(2)

    pairs = (
        (hid_hbm, hid), (lists_hbm, lists), (sent_hbm, sent), (targets_hbm, targets),
        (counts_hbm, counts), (emb_hbm, table),
    )
    loads = [
        pltpu.make_async_copy(src, dst, sem_load.at[i]) for i, (src, dst) in enumerate(pairs)
    ]
    for load in loads:
        load.start()

    barrier = pltpu.get_barrier_semaphore()
    near = [at_x(k, f) for k, f in XC_PEERS]
    near += [at_z(s * k) for k in range(1, REACH + 1) for s in (1, -1)]
    near += [at_y(k) for k in range(1, NY)]
    for peer in near:
        pl.semaphore_signal(barrier, inc=1, device_id=peer, device_id_type=MESH)

    for load in loads[:4]:
        load.wait()
    lane = lax.broadcasted_iota(I32, (1, TOK), 1)
    lane_x, lane_z = (lane >> 4) & 3, (z + (lane >> 6)) & (NZ - 1)
    place = ((lane_z & 1) << 6) + (((lane >> 3) & 1) << 5) + (lane & 7)
    ids = targets[...]
    digits = jnp.concatenate([ids & 255, (ids >> 8) & 255, ids >> 16], axis=0).astype(F32).astype(BF16)
    here = lax.broadcasted_iota(I32, (32, TOK), 0) == lane_x * 8 + (lane_z >> 1)

    def plane_targets(py):
        pick = lax.broadcasted_iota(I32, (128, TOK), 0) == place + py * 8
        found = dot(digits, pick.astype(F32).astype(BF16), ((1,), (0,)))
        value = found[:32] + found[32:64] * 256.0 + found[64:] * 65536.0
        return jnp.sum(jnp.where(here, value, 0.0), axis=0, keepdims=True).astype(I32)

    own_targets = plane_targets(y)
    other_targets = plane_targets(lax.rem(y + 2, NY))
    sentence = lax.broadcasted_iota(I32, (64, TOK), 0) == lane_x * NZ + lane_z
    lang = dot(
        jnp.broadcast_to(sent[...], (8, 64)).astype(F32).astype(BF16),
        sentence.astype(F32).astype(BF16), ((1,), (0,)),
    )[0:1].astype(I32)
    lists_now = lists[...]
    member = jnp.concatenate(
        [jnp.any(lists_now == v * NB + b, axis=1, keepdims=True).astype(F32) for b in range(NB)],
        axis=1,
    )
    hit = (lax.broadcasted_iota(I32, (lists.shape[0], TOK), 0) == lang).astype(F32)
    allowed[...] = dot(member, hit, ((0,), (0,)))
    rows[0:1, :] = own_targets
    rows[1:2, :] = other_targets

    mine = hid[...].astype(F32)
    low, high = mine[:, :HALF], mine[:, HALF:]
    swap[0] = jnp.where(c == 0, high, low)
    kept = jnp.where(c == 0, low, high)
    pl.semaphore_wait(barrier, len(near))
    trade = remote(swap.at[0], swap.at[1], sem_swap.at[0], sem_swap.at[1], partner)
    trade.start()
    trade.wait_recv()
    first = jnp.where(c == 0, kept, swap[1])
    second = jnp.where(c == 0, swap[1], kept)

    half = pl.ds(pl.multiple_of(c * HALF, HALF), HALF)

    def spot(ref, slot, px):
        return ref.at[pl.ds(pl.multiple_of((slot % NZ) * 64 + px * 16, 16), 16), half]

    def chunk_of(ref, g):
        return ref.at[pl.ds(g * CHUNK, CHUNK), half]

    tokens[pl.ds(pl.multiple_of(x * 16, 16), 16), half] = (
        jnp.concatenate([first, second], axis=0).astype(BF16)
    )

    def z_send(k, step):
        remote(
            spot(tokens, k, x), spot(tokens, k - step, x),
            sem_z_send, sem_z.at[(k - step) % NZ], at_z(step),
        ).start()

    def share(k, px):
        slot = k % NZ
        g = slot // 4
        block = spot(tokens, slot, px)
        remote(block, block, sem_c_send.at[g], sem_c.at[g], partner).start()
        remote(block, spot(tokens2, slot, px), sem_y_send.at[g], sem_y.at[g], across).start()

    def z_step(k):
        slot = k % NZ
        block = spot(tokens, slot, x)
        if k:
            remote(block, block, sem_z_send, sem_z.at[slot], partner).wait_recv()
        if k == -REACH:
            for step in range(1, NZ // 2 - REACH + 1):
                z_send(k, step)
        if k == REACH:
            for step in range(1, NZ // 2 - REACH):
                z_send(k, -step)
        for j, xk in enumerate(XPEERS):
            seen = XPEERS.index(NX - xk)
            remote(block, block, sem_x_send.at[j], sem_x.at[seen, slot], at_x(xk)).start()
        share(k, x)

    def x_steps(g):
        for slot in range(4 * g, 4 * g + 4) if g < 2 else range(4 * g + 3, 4 * g - 1, -1):
            for j, xk in enumerate(XPEERS):
                px = lax.rem(x + xk, NX)
                block = spot(tokens, slot, px)
                remote(block, block, sem_x_send.at[j], sem_x.at[j, slot], partner).wait_recv()
                share(slot, px)

    def rows_of(g):
        return slice(g * CHUNK, (g + 1) * CHUNK)

    word = lax.broadcasted_iota(I32, (BLK, CHUNK), 0)

    def chunk_logits(g):
        whole = chunk_of(tokens, g)
        remote(whole, whole, sem_c_send.at[g], sem_c.at[g], partner).wait_recv()
        at = rows_of(g)
        held = tokens[at, :]
        target = rows[0:1, at] - v * ROWS
        top = jnp.full((1, CHUNK), FILL, F32)
        hit_logit = jnp.zeros((1, CHUNK), F32)
        for b in range(NB):
            score = dot(table[b * BLK:(b + 1) * BLK, :], held, ((1,), (1,))) - log_counts[0:1, b:b + 1]
            score = jnp.where(allowed[b:b + 1, at] > 0.5, score, FILL)
            logits[b * BLK:(b + 1) * BLK, at] = score
            top = jnp.maximum(top, jnp.max(score, axis=0, keepdims=True))
            hit_logit += jnp.sum(jnp.where(word + b * BLK == target, score, 0.0), axis=0, keepdims=True)
        total = jnp.zeros((1, CHUNK), F32)
        for b in range(NB):
            weight = jnp.exp(logits[b * BLK:(b + 1) * BLK, at] - top)
            logits[b * BLK:(b + 1) * BLK, at] = weight
            total += jnp.sum(weight, axis=0, keepdims=True)
        peaks[g] = top
        local = top + jnp.log(total)
        for r in range(2):
            lse_out[2 * g + r] = local[:, r * 128:(r + 1) * 128]
            tgt_out[2 * g + r] = hit_logit[:, r * 128:(r + 1) * 128]
        for i, (k, f) in enumerate(XC_PEERS):
            remote(
                lse_out.at[pl.ds(2 * g, 2)], s1.at[my_slot, pl.ds(2 * g, 2)],
                sem_s1s.at[g, i], sem_s1.at[g, my_slot], at_x(k, f),
            ).start()

    my_slot = x * 2 + c

    def slot_of(k, f):
        return lax.rem(x + k, NX) * 2 + ((1 - c) if f else c)

    far_first = sorted(range(1, NZ), key=lambda k: -min(k, NZ - k))

    def chunk_totals(g):
        two = pl.ds(2 * g, 2)
        parts = [lse_out[two]]
        for i, (k, f) in enumerate(XC_PEERS):
            there = slot_of(k, f)
            remote(
                lse_out.at[two], s1.at[there, two], sem_s1s.at[g, i], sem_s1.at[g, there], partner
            ).wait_recv()
            parts.append(s1[there, two])
        l1_out[two] = merge(parts)
        for k in far_first:
            remote(
                l1_out.at[two], s2.at[z, two], sem_s2s.at[g, k], sem_s2.at[g, z], at_z(k)
            ).start()

    peaks = [None] * 4

    for k in range(REACH, 0, -1):
        z_send(0, k)
        z_send(0, -k)
    for k in ZORDER:
        z_step(k)
    loads[4].wait()
    loads[5].wait()
    log_counts = jnp.log(counts[...].astype(F32))

    ca, cb, cc, cd = CHUNKS
    x_steps(ca)
    x_steps(cb)
    chunk_logits(ca)
    x_steps(cc)
    chunk_logits(cb)
    chunk_totals(ca)
    x_steps(cd)
    chunk_logits(cc)
    chunk_totals(cb)
    chunk_logits(cd)
    chunk_totals(cc)
    chunk_totals(cd)

    for i, (k, f) in enumerate(XC_PEERS):
        remote(tgt_out, t1.at[my_slot], sem_t1s.at[i], sem_t1.at[my_slot], at_x(k, f)).start()

    up = lax.rem(y + 1, NY) * 2
    down = lax.rem(y + 3, NY) * 2 + 1
    held_blocks = (up, down, y * 2, y * 2 + 1)
    peaks2 = [None] * 4

    def pass_on(g):
        whole = chunk_of(tokens2, g)
        remote(whole, whole, sem_y_send.at[g], sem_y.at[g], partner).wait_recv()
        remote(whole, whole, sem_c2_send.at[g], sem_c2.at[g], partner).start()

    block_lane = lax.broadcasted_iota(I32, (1, NB), 1)
    block_row = lax.broadcasted_iota(I32, (NB, CHUNK), 0)

    def other_logits(g):
        whole = chunk_of(tokens2, g)
        remote(whole, whole, sem_c2_send.at[g], sem_c2.at[g], partner).wait_recv()
        at = rows_of(g)
        held = tokens2[at, :]
        may = allowed[:, at]
        top = jnp.full((1, CHUNK), FILL, F32)
        for i, b in enumerate(held_blocks):
            entry = table[pl.ds(pl.multiple_of(b * BLK, BLK), BLK), :]
            less = jnp.sum(jnp.where(block_lane == b, log_counts, 0.0), axis=1, keepdims=True)
            ok = jnp.sum(jnp.where(block_row == b, may, 0.0), axis=0, keepdims=True) > 0.5
            score = jnp.where(ok, dot(entry, held, ((1,), (1,))) - less, FILL)
            logits2[i * BLK:(i + 1) * BLK, at] = score
            top = jnp.maximum(top, jnp.max(score, axis=0, keepdims=True))
        for i in range(4):
            logits2[i * BLK:(i + 1) * BLK, at] = jnp.exp(logits2[i * BLK:(i + 1) * BLK, at] - top)
        peaks2[g] = top

    pass_on(ca)
    pass_on(cb)
    other_logits(ca)
    pass_on(cc)
    other_logits(cb)
    pass_on(cd)
    other_logits(cc)

    first_half = lax.broadcasted_iota(I32, (1, 128), 1) < 64
    parts = [[l1_out[r]] for r in range(8)]
    for k in far_first[::-1]:
        there = lax.rem(z + k, NZ)
        for g in CHUNKS:
            two = pl.ds(2 * g, 2)
            remote(
                l1_out.at[two], s2.at[there, two], sem_s2s.at[g, k], sem_s2.at[g, there], partner
            ).wait_recv()
        theirs = [s2[there, r] for r in range(8)]
        if k % 2:
            turned = [pltpu.roll(t, 64, 1) for t in theirs]
        for r in range(8):
            if k % 2:
                before = ((2 * r - k - 1) // 2) % 8
                parts[r].append(jnp.where(first_half, turned[before], turned[(before + 1) % 8]))
            else:
                parts[r].append(theirs[(r - k // 2) % 8])
    total_rows = [merge(p) for p in parts]
    for r in range(8):
        l_out[r] = total_rows[r]
    tell = remote(l_out, l_in, sem_l.at[0], sem_l.at[1], across)
    tell.start()
    other_logits(cd)

    scale = jnp.exp(jnp.concatenate(peaks, axis=1) - jnp.concatenate(total_rows, axis=1))
    deep = lax.broadcasted_iota(I32, (BLK, TOK), 0)
    own_row = rows[0:1, :] - v * ROWS
    other_row = rows[1:2, :] - v * ROWS

    def fill_probs(source, at, b, n, factor, target):
        weight = source[pl.ds(pl.multiple_of(at * BLK, BLK), BLK), :] * factor
        weight = weight - (deep + b * BLK == target).astype(F32)
        probs[n * BLK:(n + 1) * BLK, :] = weight.astype(BF16)

    for n, b in enumerate(held_blocks):
        fill_probs(logits, b, b, n, scale, own_row)
    sums[...] = dot(probs[...], tokens[...], ((1,), (0,)))

    tell.wait_recv()
    other_total = jnp.concatenate([l_in[r] for r in range(8)], axis=1)
    scale2 = jnp.exp(jnp.concatenate(peaks2, axis=1) - other_total)
    for n, b in enumerate(held_blocks):
        fill_probs(logits2, n, b, n, scale2, other_row)
    for n, to in ((0, at_y(1)), (1, at_y(3))):
        at = slice(n * BLK, (n + 1) * BLK)
        send_buf[n] = (sums[at, :] + dot(probs[at, :], tokens2[...], ((1,), (0,)))).astype(BF16)
        remote(send_buf.at[n], recv_buf.at[n], sem_rs.at[n], sem_rr.at[n], to).start()

    tsum = tgt_out[...]
    for i, (k, f) in enumerate(XC_PEERS):
        there = slot_of(k, f)
        remote(tgt_out, t1.at[there], sem_t1s.at[i], sem_t1.at[there], partner).wait_recv()
        tsum = tsum + t1[there]
    tsum_out[...] = tsum
    for k in far_first:
        remote(tsum_out.at[k // 2], t2.at[z], sem_t2s.at[k], sem_t2.at[z], at_z(k)).start()

    sums[2 * BLK:, :] += dot(probs[2 * BLK:, :], tokens2[...], ((1,), (0,)))

    tgt = tsum_out[0]
    for k in far_first[::-1]:
        there = lax.rem(z + k, NZ)
        remote(tsum_out.at[0], t2.at[there], sem_t2s.at[k], sem_t2.at[there], partner).wait_recv()
        theirs = t2[there]
        tgt = tgt + (pltpu.roll(theirs, 64, 1) if k % 2 else theirs)
    lane0 = x * 16 + c * 8
    loss = jnp.broadcast_to(l_out[0] - tgt, (8, 128))
    loss_ref[...] = pltpu.roll(loss, lax.rem(128 - lane0, 128), 1)

    for n in range(2):
        remote(send_buf.at[n], recv_buf.at[n], sem_rs.at[n], sem_rr.at[n], partner).wait_recv()
        at = slice(n * BLK, (n + 1) * BLK)
        out_buf[at, :] = (sums[(2 + n) * BLK:(3 + n) * BLK, :] + recv_buf[n].astype(F32)).astype(BF16)
    put = pltpu.make_async_copy(out_buf, grad_ref, sem_out)
    put.start()

    trade.wait_send()
    tell.wait_send()
    block = tokens.at[pl.ds(0, 240), pl.ds(0, HALF)]
    remote(block, block, sem_z_send, sem_z.at[0], partner).wait_send()
    whole = chunk_of(tokens, 0)
    for j in range(3):
        remote(whole, whole, sem_x_send.at[j], sem_x.at[j, 0], partner).wait_send()
    for g in range(4):
        remote(whole, whole, sem_c_send.at[g], sem_c.at[g], partner).wait_send()
        remote(whole, whole, sem_y_send.at[g], sem_y.at[g], partner).wait_send()
        remote(whole, whole, sem_c2_send.at[g], sem_c2.at[g], partner).wait_send()
        two = pl.ds(0, 2)
        for i in range(7):
            remote(lse_out.at[two], s1.at[0, two], sem_s1s.at[g, i], sem_s1.at[g, 0], partner).wait_send()
        for k in range(1, NZ):
            remote(l1_out.at[two], s2.at[0, two], sem_s2s.at[g, k], sem_s2.at[g, 0], partner).wait_send()
    for i in range(7):
        remote(tgt_out, t1.at[0], sem_t1s.at[i], sem_t1.at[0], partner).wait_send()
    for k in range(1, NZ):
        remote(tsum_out.at[0], t2.at[0], sem_t2s.at[k], sem_t2.at[0], partner).wait_send()
    for n in range(2):
        remote(send_buf.at[n], recv_buf.at[n], sem_rs.at[n], sem_rr.at[n], partner).wait_send()
    put.wait()


def body(hidden, embedding, block_counts, lang_blocks, sent_lang, targets):
    vmem, dma = pltpu.VMEM, pltpu.SemaphoreType.DMA
    anywhere = pl.BlockSpec(memory_space=pl.ANY)
    loss, grad = pl.pallas_call(
        kernel,
        out_shape=(
            jax.ShapeDtypeStruct((8, 128), F32),
            jax.ShapeDtypeStruct((QROWS, D), BF16),
        ),
        in_specs=[anywhere] * 6,
        out_specs=(pl.BlockSpec(memory_space=pltpu.VMEM), anywhere),
        scratch_shapes=[
            vmem(hidden.shape, BF16),
            vmem((ROWS, D), BF16),
            vmem((1, NB), I32),
            vmem(lang_blocks.shape, I32),
            vmem((1, 64), I32),
            vmem((32, 128), I32),
            vmem((TOK, D), BF16),
            vmem((TOK, D), BF16),
            vmem((ROWS, TOK), F32),
            vmem((4 * BLK, TOK), F32),
            vmem((4 * BLK, TOK), BF16),
            vmem((4 * BLK, D), F32),
            vmem((2, 8, HALF), F32),
            vmem((NB, TOK), F32),
            vmem((8, TOK), I32),
            vmem((8, 8, 1, 128), F32),
            vmem((NZ, 8, 1, 128), F32),
            vmem((8, 8, 1, 128), F32),
            vmem((NZ, 1, 128), F32),
            vmem((8, 1, 128), F32),
            vmem((8, 1, 128), F32),
            vmem((8, 1, 128), F32),
            vmem((8, 1, 128), F32),
            vmem((8, 1, 128), F32),
            vmem((8, 1, 128), F32),
            vmem((2, BLK, D), BF16),
            vmem((2, BLK, D), BF16),
            vmem((QROWS, D), BF16),
            dma((6,)), dma((2,)), dma, dma((NZ,)), dma((3,)), dma((3, NZ)),
            dma((4,)), dma((4,)), dma((4,)), dma((4,)), dma((4,)), dma((4,)),
            dma((4, 7)), dma((4, 8)), dma((4, NZ)), dma((4, NZ)),
            dma((7,)), dma((8,)), dma((NZ,)), dma((NZ,)),
            dma((2,)), dma((2,)), dma((2,)), dma,
        ],
        compiler_params=pltpu.CompilerParams(
            collective_id=0, has_side_effects=True, vmem_limit_bytes=56 << 20
        ),
    )(
        hidden, embedding, block_counts.reshape(1, NB), lang_blocks,
        sent_lang.reshape(1, 64), targets.reshape(32, 128),
    )
    return loss[0, :8], grad


def solution(mesh):
    in_specs = (P(("vocab", "batch"), None), P("vocab", None), P("vocab"), P(), P(), P())
    out_specs = (P(("vocab", "batch")), P(("vocab", "batch"), None))
    return jax.shard_map(body, mesh=mesh, in_specs=in_specs, out_specs=out_specs, check_vma=False)
```

```python
import functools

import jax
import jax.numpy as jnp
from jax import lax
from jax.experimental import pallas as pl
from jax.experimental.pallas import tpu as pltpu
from jax.sharding import PartitionSpec as P

MESH = pl.DeviceIdType.MESH
F32, BF16, I32 = jnp.float32, jnp.bfloat16, jnp.int32
NX, NZ, NY = 4, 16, 4
D = 1024
HALF = 512
ROWS = 1024
TOK = 1024
NB = 8
BLK = 128
QROWS = 256
CHUNK = 256
FILL = -3e38
REACH = 2
ZORDER = [0] + [s * k for k in range(1, 8) for s in (1, -1)] + [-8]
XPEERS = (1, 3, 2)
XC_PEERS = [(k, f) for f in (0, 1) for k in range(NX) if (k, f) != (0, 0)]
CHUNKS = (0, 3, 1, 2)


def remote(src, dst, send, recv, device):
    return pltpu.make_async_remote_copy(
        src_ref=src, dst_ref=dst, send_sem=send, recv_sem=recv,
        device_id=device, device_id_type=MESH,
    )


def merge(parts):
    top = functools.reduce(jnp.maximum, parts)
    total = functools.reduce(jnp.add, [jnp.exp(p - top) for p in parts])
    return top + jnp.log(total)


def dot(a, b, contract):
    return lax.dot_general(a, b, (contract, ((), ())), preferred_element_type=F32)


def kernel(
    hid_hbm, emb_hbm, counts_hbm, lists_hbm, sent_hbm, targets_hbm,
    loss_ref, own_ref, recv_ref,
    hid, table, counts, lists, sent, targets,
    tokens, tokens2, logits, logits2, probs, sums, swap, allowed, rows,
    s1, s2, t1, t2, lse_out, l1_out, tgt_out, tsum_out, l_out, l_in,
    send_buf,
    sem_load, sem_swap, sem_z_send, sem_z, sem_x_send, sem_x, sem_c_send, sem_c,
    sem_y_send, sem_y, sem_c2_send, sem_c2,
    sem_s1s, sem_s1, sem_s2s, sem_s2, sem_t1s, sem_t1, sem_t2s, sem_t2,
    sem_l, sem_rs, sem_rr, sem_out,
):
    v, y = lax.axis_index("vocab"), lax.axis_index("batch")
    c = lax.rem(v, 2)
    z = lax.rem(lax.div(v, 2), NZ)
    x = lax.div(v, 2 * NZ)

    def dev(px, pz, pc, py):
        return {"vocab": (px * NZ + pz) * 2 + pc, "batch": py}

    def at_z(k):
        return dev(x, lax.rem(z + k + 2 * NZ, NZ), c, y)

    def at_x(k, flip=0):
        return dev(lax.rem(x + k, NX), z, (1 - c) if flip else c, y)

    def at_y(k):
        return dev(x, z, c, lax.rem(y + k, NY))

    partner = dev(x, z, 1 - c, y)
    across = at_y(2)

    pairs = (
        (hid_hbm, hid), (lists_hbm, lists), (sent_hbm, sent), (targets_hbm, targets),
        (counts_hbm, counts), (emb_hbm, table),
    )
    loads = [
        pltpu.make_async_copy(src, dst, sem_load.at[i]) for i, (src, dst) in enumerate(pairs)
    ]
    for load in loads:
        load.start()

    barrier = pltpu.get_barrier_semaphore()
    near = [at_x(k, f) for k, f in XC_PEERS]
    near += [at_z(s * k) for k in range(1, REACH + 1) for s in (1, -1)]
    near += [at_y(k) for k in range(1, NY)]
    for peer in near:
        pl.semaphore_signal(barrier, inc=1, device_id=peer, device_id_type=MESH)

    loads[0].wait()
    mine = hid[...].astype(F32)
    low, high = mine[:, :HALF], mine[:, HALF:]
    swap[0] = jnp.where(c == 0, high, low)
    kept = jnp.where(c == 0, low, high)
    pl.semaphore_wait(barrier, len(near))
    trade = remote(swap.at[0], swap.at[1], sem_swap.at[0], sem_swap.at[1], partner)
    trade.start()
    trade.wait_recv()
    first = jnp.where(c == 0, kept, swap[1])
    second = jnp.where(c == 0, swap[1], kept)

    half = pl.ds(pl.multiple_of(c * HALF, HALF), HALF)

    def spot(ref, slot, px):
        return ref.at[pl.ds(pl.multiple_of((slot % NZ) * 64 + px * 16, 16), 16), half]

    def chunk_of(ref, g):
        return ref.at[pl.ds(g * CHUNK, CHUNK), half]

    tokens[pl.ds(pl.multiple_of(x * 16, 16), 16), half] = (
        jnp.concatenate([first, second], axis=0).astype(BF16)
    )

    def z_send(k, step):
        remote(
            spot(tokens, k, x), spot(tokens, k - step, x),
            sem_z_send, sem_z.at[(k - step) % NZ], at_z(step),
        ).start()

    def share(k, px):
        slot = k % NZ
        g = slot // 4
        block = spot(tokens, slot, px)
        remote(block, block, sem_c_send.at[g], sem_c.at[g], partner).start()
        remote(block, spot(tokens2, slot, px), sem_y_send.at[g], sem_y.at[g], across).start()

    def z_step(k):
        slot = k % NZ
        block = spot(tokens, slot, x)
        if k:
            remote(block, block, sem_z_send, sem_z.at[slot], partner).wait_recv()
        if k and k % REACH == 0:
            for step in range(1, REACH + 1):
                if k < 0 and step - k <= NZ // 2:
                    z_send(k, step)
                if k > 0 and step + k < NZ // 2:
                    z_send(k, -step)
        for j, xk in enumerate(XPEERS):
            seen = XPEERS.index(NX - xk)
            remote(block, block, sem_x_send.at[j], sem_x.at[seen, slot], at_x(xk)).start()
        share(k, x)

    def x_step(slot):
        for j, xk in enumerate(XPEERS):
            px = lax.rem(x + xk, NX)
            block = spot(tokens, slot, px)
            remote(block, block, sem_x_send.at[j], sem_x.at[j, slot], partner).wait_recv()
            share(slot, px)

    def rows_of(g):
        return slice(g * CHUNK, (g + 1) * CHUNK)

    word = lax.broadcasted_iota(I32, (BLK, CHUNK), 0)

    def chunk_logits(g):
        whole = chunk_of(tokens, g)
        remote(whole, whole, sem_c_send.at[g], sem_c.at[g], partner).wait_recv()
        at = rows_of(g)
        held = tokens[at, :]
        target = rows[0:1, at] - v * ROWS
        top = jnp.full((1, CHUNK), FILL, F32)
        hit_logit = jnp.zeros((1, CHUNK), F32)
        for b in range(NB):
            score = dot(table[b * BLK:(b + 1) * BLK, :], held, ((1,), (1,))) - log_counts[0:1, b:b + 1]
            score = jnp.where(allowed[b:b + 1, at] > 0.5, score, FILL)
            logits[b * BLK:(b + 1) * BLK, at] = score
            top = jnp.maximum(top, jnp.max(score, axis=0, keepdims=True))
            hit_logit += jnp.sum(jnp.where(word + b * BLK == target, score, 0.0), axis=0, keepdims=True)
        total = jnp.zeros((1, CHUNK), F32)
        for b in range(NB):
            weight = jnp.exp(logits[b * BLK:(b + 1) * BLK, at] - top)
            logits[b * BLK:(b + 1) * BLK, at] = weight
            total += jnp.sum(weight, axis=0, keepdims=True)
        peaks[g] = top
        local = top + jnp.log(total)
        for r in range(2):
            lse_out[2 * g + r] = local[:, r * 128:(r + 1) * 128]
            tgt_out[2 * g + r] = hit_logit[:, r * 128:(r + 1) * 128]
        for i, (k, f) in enumerate(XC_PEERS):
            remote(
                lse_out.at[pl.ds(2 * g, 2)], s1.at[my_slot, pl.ds(2 * g, 2)],
                sem_s1s.at[g, i], sem_s1.at[g, my_slot], at_x(k, f),
            ).start()

    my_slot = x * 2 + c

    def slot_of(k, f):
        return lax.rem(x + k, NX) * 2 + ((1 - c) if f else c)

    far_first = sorted(range(1, NZ), key=lambda k: -min(k, NZ - k))

    def chunk_totals(g):
        two = pl.ds(2 * g, 2)
        parts = [lse_out[two]]
        for i, (k, f) in enumerate(XC_PEERS):
            there = slot_of(k, f)
            remote(
                lse_out.at[two], s1.at[there, two], sem_s1s.at[g, i], sem_s1.at[g, there], partner
            ).wait_recv()
            parts.append(s1[there, two])
        l1_out[two] = merge(parts)
        for k in far_first:
            remote(
                l1_out.at[two], s2.at[z, two], sem_s2s.at[g, k], sem_s2.at[g, z], at_z(k)
            ).start()

    peaks = [None] * 4

    for k in range(REACH, 0, -1):
        z_send(0, k)
        z_send(0, -k)
    z_step(0)

    for k in ZORDER[1:5]:
        z_step(k)

    for load in loads[1:4]:
        load.wait()
    lane = lax.broadcasted_iota(I32, (1, TOK), 1)
    lane_x, lane_z = (lane >> 4) & 3, (z + (lane >> 6)) & (NZ - 1)
    place = ((lane_z & 1) << 6) + (((lane >> 3) & 1) << 5) + (lane & 7)
    ids = targets[...]
    digits = jnp.concatenate([ids & 255, (ids >> 8) & 255, ids >> 16], axis=0).astype(F32).astype(BF16)
    here = lax.broadcasted_iota(I32, (32, TOK), 0) == lane_x * 8 + (lane_z >> 1)

    def plane_targets(py):
        pick = lax.broadcasted_iota(I32, (128, TOK), 0) == place + py * 8
        found = dot(digits, pick.astype(F32).astype(BF16), ((1,), (0,)))
        value = found[:32] + found[32:64] * 256.0 + found[64:] * 65536.0
        return jnp.sum(jnp.where(here, value, 0.0), axis=0, keepdims=True).astype(I32)

    own_targets = plane_targets(y)
    other_targets = plane_targets(lax.rem(y + 2, NY))
    rows[0:1, :] = own_targets
    rows[1:2, :] = other_targets

    for k in ZORDER[5:9]:
        z_step(k)
    x_step(0)

    sentence = lax.broadcasted_iota(I32, (64, TOK), 0) == lane_x * NZ + lane_z
    lang = dot(
        jnp.broadcast_to(sent[...], (8, 64)).astype(F32).astype(BF16),
        sentence.astype(F32).astype(BF16), ((1,), (0,)),
    )[0:1].astype(I32)
    lists_now = lists[...]
    member = jnp.concatenate(
        [jnp.any(lists_now == v * NB + b, axis=0, keepdims=True).astype(F32) for b in range(NB)],
        axis=0,
    )
    hit = (lax.broadcasted_iota(I32, (lists.shape[1], TOK), 0) == lang).astype(F32)
    allowed[...] = dot(member, hit, ((1,), (0,)))

    for slot in (1, 15, 2, 14):
        x_step(slot)
    for k in ZORDER[9:13]:
        z_step(k)
    for slot in (3, 13, 4, 12):
        x_step(slot)
    for k in ZORDER[13:]:
        z_step(k)
    loads[4].wait()
    loads[5].wait()
    log_counts = jnp.log(counts[...].astype(F32))

    ca, cb, cc, cd = CHUNKS
    chunk_logits(ca)
    for slot in (5, 11, 6, 10):
        x_step(slot)
    chunk_logits(cb)
    chunk_totals(ca)
    for slot in (7, 9, 8):
        x_step(slot)
    chunk_logits(cc)
    chunk_totals(cb)
    chunk_logits(cd)
    chunk_totals(cc)
    chunk_totals(cd)

    for i, (k, f) in enumerate(XC_PEERS):
        remote(tgt_out, t1.at[my_slot], sem_t1s.at[i], sem_t1.at[my_slot], at_x(k, f)).start()

    up = lax.rem(y + 1, NY) * 2
    down = lax.rem(y + 3, NY) * 2 + 1
    held_blocks = (up, down, y * 2, y * 2 + 1)
    peaks2 = [None] * 4

    def pass_on(g):
        whole = chunk_of(tokens2, g)
        remote(whole, whole, sem_y_send.at[g], sem_y.at[g], partner).wait_recv()
        remote(whole, whole, sem_c2_send.at[g], sem_c2.at[g], partner).start()

    block_lane = lax.broadcasted_iota(I32, (1, NB), 1)
    block_row = lax.broadcasted_iota(I32, (NB, CHUNK), 0)

    def other_logits(g):
        whole = chunk_of(tokens2, g)
        remote(whole, whole, sem_c2_send.at[g], sem_c2.at[g], partner).wait_recv()
        at = rows_of(g)
        held = tokens2[at, :]
        may = allowed[:, at]
        top = jnp.full((1, CHUNK), FILL, F32)
        for i, b in enumerate(held_blocks):
            entry = table[pl.ds(pl.multiple_of(b * BLK, BLK), BLK), :]
            less = jnp.sum(jnp.where(block_lane == b, log_counts, 0.0), axis=1, keepdims=True)
            ok = jnp.sum(jnp.where(block_row == b, may, 0.0), axis=0, keepdims=True) > 0.5
            score = jnp.where(ok, dot(entry, held, ((1,), (1,))) - less, FILL)
            logits2[i * BLK:(i + 1) * BLK, at] = score
            top = jnp.maximum(top, jnp.max(score, axis=0, keepdims=True))
        for i in range(4):
            logits2[i * BLK:(i + 1) * BLK, at] = jnp.exp(logits2[i * BLK:(i + 1) * BLK, at] - top)
        peaks2[g] = top

    pass_on(ca)
    pass_on(cb)
    other_logits(ca)
    pass_on(cc)
    other_logits(cb)
    pass_on(cd)
    other_logits(cc)
    tsum = tgt_out[...]
    for i, (k, f) in enumerate(XC_PEERS):
        there = slot_of(k, f)
        remote(tgt_out, t1.at[there], sem_t1s.at[i], sem_t1.at[there], partner).wait_recv()
        tsum = tsum + t1[there]
    tsum_out[...] = tsum
    for k in far_first:
        remote(tsum_out.at[k // 2], t2.at[z], sem_t2s.at[k], sem_t2.at[z], at_z(k)).start()
    other_logits(cd)

    first_half = lax.broadcasted_iota(I32, (1, 128), 1) < 64
    parts = [[l1_out[r]] for r in range(8)]
    for k in far_first[::-1]:
        there = lax.rem(z + k, NZ)
        for g in CHUNKS:
            two = pl.ds(2 * g, 2)
            remote(
                l1_out.at[two], s2.at[there, two], sem_s2s.at[g, k], sem_s2.at[g, there], partner
            ).wait_recv()
        theirs = [s2[there, r] for r in range(8)]
        if k % 2:
            turned = [pltpu.roll(t, 64, 1) for t in theirs]
        for r in range(8):
            if k % 2:
                before = ((2 * r - k - 1) // 2) % 8
                parts[r].append(jnp.where(first_half, turned[before], turned[(before + 1) % 8]))
            else:
                parts[r].append(theirs[(r - k // 2) % 8])
    total_rows = [merge(p) for p in parts]
    for r in range(8):
        l_out[r] = total_rows[r]
    tell = remote(l_out, l_in, sem_l.at[0], sem_l.at[1], across)
    tell.start()

    scale = jnp.exp(jnp.concatenate(peaks, axis=1) - jnp.concatenate(total_rows, axis=1))
    deep = lax.broadcasted_iota(I32, (BLK, TOK), 0)
    own_row = rows[0:1, :] - v * ROWS
    other_row = rows[1:2, :] - v * ROWS

    def fill_probs(source, at, b, n, factor, target):
        weight = source[pl.ds(pl.multiple_of(at * BLK, BLK), BLK), :] * factor
        weight = weight - (deep + b * BLK == target).astype(F32)
        probs[n * BLK:(n + 1) * BLK, :] = weight.astype(BF16)

    for n, b in enumerate(held_blocks):
        fill_probs(logits, b, b, n, scale, own_row)
    sums[...] = dot(probs[...], tokens[...], ((1,), (0,)))

    tell.wait_recv()
    other_total = jnp.concatenate([l_in[r] for r in range(8)], axis=1)
    scale2 = jnp.exp(jnp.concatenate(peaks2, axis=1) - other_total)
    for n, to in ((0, at_y(1)), (1, at_y(3))):
        fill_probs(logits2, n, held_blocks[n], n, scale2, other_row)
        at = slice(n * BLK, (n + 1) * BLK)
        send_buf[n] = (sums[at, :] + dot(probs[at, :], tokens2[...], ((1,), (0,)))).astype(BF16)
        remote(send_buf.at[n], recv_ref.at[pl.ds(n * BLK, BLK)], sem_rs.at[n], sem_rr.at[n], to).start()
    for n in (2, 3):
        fill_probs(logits2, n, held_blocks[n], n, scale2, other_row)
    sums[2 * BLK:, :] += dot(probs[2 * BLK:, :], tokens2[...], ((1,), (0,)))
    put = pltpu.make_async_copy(sums.at[pl.ds(2 * BLK, QROWS)], own_ref, sem_out)
    put.start()

    tgt = tsum_out[0]
    for k in far_first[::-1]:
        there = lax.rem(z + k, NZ)
        remote(tsum_out.at[0], t2.at[there], sem_t2s.at[k], sem_t2.at[there], partner).wait_recv()
        theirs = t2[there]
        tgt = tgt + (pltpu.roll(theirs, 64, 1) if k % 2 else theirs)
    lane0 = x * 16 + c * 8
    loss = jnp.broadcast_to(l_out[0] - tgt, (8, 128))
    loss_ref[...] = pltpu.roll(loss, lax.rem(128 - lane0, 128), 1)

    for n in range(2):
        part = recv_ref.at[pl.ds(n * BLK, BLK)]
        remote(send_buf.at[n], part, sem_rs.at[n], sem_rr.at[n], partner).wait_recv()

    trade.wait_send()
    tell.wait_send()
    block = tokens.at[pl.ds(0, 240), pl.ds(0, HALF)]
    remote(block, block, sem_z_send, sem_z.at[0], partner).wait_send()
    whole = chunk_of(tokens, 0)
    for j in range(3):
        remote(whole, whole, sem_x_send.at[j], sem_x.at[j, 0], partner).wait_send()
    for g in range(4):
        remote(whole, whole, sem_c_send.at[g], sem_c.at[g], partner).wait_send()
        remote(whole, whole, sem_y_send.at[g], sem_y.at[g], partner).wait_send()
        remote(whole, whole, sem_c2_send.at[g], sem_c2.at[g], partner).wait_send()
        two = pl.ds(0, 2)
        for i in range(7):
            remote(lse_out.at[two], s1.at[0, two], sem_s1s.at[g, i], sem_s1.at[g, 0], partner).wait_send()
        for k in range(1, NZ):
            remote(l1_out.at[two], s2.at[0, two], sem_s2s.at[g, k], sem_s2.at[g, 0], partner).wait_send()
    for i in range(7):
        remote(tgt_out, t1.at[0], sem_t1s.at[i], sem_t1.at[0], partner).wait_send()
    for k in range(1, NZ):
        remote(tsum_out.at[0], t2.at[0], sem_t2s.at[k], sem_t2.at[0], partner).wait_send()
    for n in range(2):
        part = recv_ref.at[pl.ds(n * BLK, BLK)]
        remote(send_buf.at[n], part, sem_rs.at[n], sem_rr.at[n], partner).wait_send()
    put.wait()


def body(hidden, embedding, block_counts, lang_blocks, sent_lang, targets):
    vmem, dma = pltpu.VMEM, pltpu.SemaphoreType.DMA
    anywhere = pl.BlockSpec(memory_space=pl.ANY)
    loss, own, received = pl.pallas_call(
        kernel,
        out_shape=(
            jax.ShapeDtypeStruct((8, 128), F32),
            jax.ShapeDtypeStruct((QROWS, D), F32),
            jax.ShapeDtypeStruct((QROWS, D), BF16),
        ),
        in_specs=[anywhere] * 6,
        out_specs=(pl.BlockSpec(memory_space=pltpu.VMEM), anywhere, anywhere),
        scratch_shapes=[
            vmem(hidden.shape, BF16),
            vmem((ROWS, D), BF16),
            vmem((1, NB), I32),
            vmem(lang_blocks.shape[::-1], I32),
            vmem((1, 64), I32),
            vmem((32, 128), I32),
            vmem((TOK, D), BF16),
            vmem((TOK, D), BF16),
            vmem((ROWS, TOK), F32),
            vmem((4 * BLK, TOK), F32),
            vmem((4 * BLK, TOK), BF16),
            vmem((4 * BLK, D), F32),
            vmem((2, 8, HALF), F32),
            vmem((NB, TOK), F32),
            vmem((8, TOK), I32),
            vmem((8, 8, 1, 128), F32),
            vmem((NZ, 8, 1, 128), F32),
            vmem((8, 8, 1, 128), F32),
            vmem((NZ, 1, 128), F32),
            vmem((8, 1, 128), F32),
            vmem((8, 1, 128), F32),
            vmem((8, 1, 128), F32),
            vmem((8, 1, 128), F32),
            vmem((8, 1, 128), F32),
            vmem((8, 1, 128), F32),
            vmem((2, BLK, D), BF16),
            dma((6,)), dma((2,)), dma, dma((NZ,)), dma((3,)), dma((3, NZ)),
            dma((4,)), dma((4,)), dma((4,)), dma((4,)), dma((4,)), dma((4,)),
            dma((4, 7)), dma((4, 8)), dma((4, NZ)), dma((4, NZ)),
            dma((7,)), dma((8,)), dma((NZ,)), dma((NZ,)),
            dma((2,)), dma((2,)), dma((2,)), dma,
        ],
        compiler_params=pltpu.CompilerParams(
            collective_id=0, has_side_effects=True, vmem_limit_bytes=54 << 20
        ),
    )(
        hidden, embedding, block_counts.reshape(1, NB), lang_blocks.T,
        sent_lang.reshape(1, 64), targets.reshape(32, 128),
    )
    return loss[0, :8], (own + received.astype(F32)).astype(BF16)


def solution(mesh):
    in_specs = (P(("vocab", "batch"), None), P("vocab", None), P("vocab"), P(), P(), P())
    out_specs = (P(("vocab", "batch")), P(("vocab", "batch"), None))
    return jax.shard_map(body, mesh=mesh, in_specs=in_specs, out_specs=out_specs, check_vma=False)
```

```python
import functools

import jax
import jax.numpy as jnp
from jax import lax
from jax.experimental import pallas as pl
from jax.experimental.pallas import tpu as pltpu
from jax.sharding import PartitionSpec as P

MESH = pl.DeviceIdType.MESH
F32, BF16, I32 = jnp.float32, jnp.bfloat16, jnp.int32
NX, NZ, NY = 4, 16, 4
D = 1024
HALF = 512
ROWS = 1024
TOK = 1024
NB = 8
BLK = 128
QROWS = 256
CHUNK = 256
FILL = -3e38
REACH = 2
ZORDER = [0] + [s * k for k in range(1, 8) for s in (1, -1)] + [-8]
XPEERS = (1, 3, 2)
XC_PEERS = [(k, f) for f in (0, 1) for k in range(NX) if (k, f) != (0, 0)]
CHUNKS = (0, 3, 1, 2)


def remote(src, dst, send, recv, device):
    return pltpu.make_async_remote_copy(
        src_ref=src, dst_ref=dst, send_sem=send, recv_sem=recv,
        device_id=device, device_id_type=MESH,
    )


def merge(parts):
    top = functools.reduce(jnp.maximum, parts)
    total = functools.reduce(jnp.add, [jnp.exp(p - top) for p in parts])
    return top + jnp.log(total)


def dot(a, b, contract):
    return lax.dot_general(a, b, (contract, ((), ())), preferred_element_type=F32)


def kernel(
    hid_hbm, emb_hbm, counts_hbm, lists_hbm, sent_hbm, targets_hbm,
    loss_ref, own_ref, recv_ref,
    hid, table, table2, counts, lists, sent, targets,
    tokens, tokens2, logits, logits2, probs, sums, swap, allowed, rows,
    s1, s2, t1, t2, lse_out, l1_out, tgt_out, tsum_out, l_out, l_in,
    send_buf,
    sem_load, sem_swap, sem_z_send, sem_z, sem_x_send, sem_x, sem_c_send, sem_c,
    sem_y_send, sem_y, sem_c2_send, sem_c2,
    sem_s1s, sem_s1, sem_s2s, sem_s2, sem_t1s, sem_t1, sem_t2s, sem_t2,
    sem_l, sem_rs, sem_rr, sem_out,
):
    v, y = lax.axis_index("vocab"), lax.axis_index("batch")
    c = lax.rem(v, 2)
    z = lax.rem(lax.div(v, 2), NZ)
    x = lax.div(v, 2 * NZ)

    def dev(px, pz, pc, py):
        return {"vocab": (px * NZ + pz) * 2 + pc, "batch": py}

    def at_z(k):
        return dev(x, lax.rem(z + k + 2 * NZ, NZ), c, y)

    def at_x(k, flip=0):
        return dev(lax.rem(x + k, NX), z, (1 - c) if flip else c, y)

    def at_y(k):
        return dev(x, z, c, lax.rem(y + k, NY))

    partner = dev(x, z, 1 - c, y)
    across = at_y(2)

    pairs = (
        (hid_hbm, hid), (lists_hbm, lists), (sent_hbm, sent), (targets_hbm, targets),
        (counts_hbm, counts), (emb_hbm, table),
    )
    loads = [
        pltpu.make_async_copy(src, dst, sem_load.at[i]) for i, (src, dst) in enumerate(pairs)
    ]
    for load in loads:
        load.start()

    barrier = pltpu.get_barrier_semaphore()
    near = [at_x(k, f) for k, f in XC_PEERS]
    near += [at_z(s * k) for k in range(1, REACH + 1) for s in (1, -1)]
    near += [at_y(k) for k in range(1, NY)]
    for peer in near:
        pl.semaphore_signal(barrier, inc=1, device_id=peer, device_id_type=MESH)

    loads[0].wait()
    mine = hid[...].astype(F32)
    low, high = mine[:, :HALF], mine[:, HALF:]
    swap[0] = jnp.where(c == 0, high, low)
    kept = jnp.where(c == 0, low, high)
    for load in loads[1:4]:
        load.wait()
    lane = lax.broadcasted_iota(I32, (1, TOK), 1)
    lane_x, lane_z = (lane >> 4) & 3, (z + (lane >> 6)) & (NZ - 1)
    place = ((lane_z & 1) << 6) + (((lane >> 3) & 1) << 5) + (lane & 7)
    ids = targets[...]
    digits = jnp.concatenate([ids & 255, (ids >> 8) & 255, ids >> 16], axis=0).astype(F32).astype(BF16)
    here = lax.broadcasted_iota(I32, (32, TOK), 0) == lane_x * 8 + (lane_z >> 1)

    def plane_targets(py):
        pick = lax.broadcasted_iota(I32, (128, TOK), 0) == place + py * 8
        found = dot(digits, pick.astype(F32).astype(BF16), ((1,), (0,)))
        value = found[:32] + found[32:64] * 256.0 + found[64:] * 65536.0
        return jnp.sum(jnp.where(here, value, 0.0), axis=0, keepdims=True).astype(I32)

    own_targets = plane_targets(y)
    other_targets = plane_targets(lax.rem(y + 2, NY))
    rows[0:1, :] = own_targets
    rows[1:2, :] = other_targets
    sentence = lax.broadcasted_iota(I32, (64, TOK), 0) == lane_x * NZ + lane_z
    lang = dot(
        jnp.broadcast_to(sent[...], (8, 64)).astype(F32).astype(BF16),
        sentence.astype(F32).astype(BF16), ((1,), (0,)),
    )[0:1].astype(I32)
    lists_now = lists[...]
    member = jnp.concatenate(
        [jnp.any(lists_now == v * NB + b, axis=0, keepdims=True).astype(F32) for b in range(NB)],
        axis=0,
    )
    hit = (lax.broadcasted_iota(I32, (lists.shape[1], TOK), 0) == lang).astype(F32)
    allowed[...] = dot(member, hit, ((1,), (0,)))
    loads[4].wait()
    loads[5].wait()
    log_counts = jnp.log(counts[...].astype(F32))
    up = lax.rem(y + 1, NY) * 2
    down = lax.rem(y + 3, NY) * 2 + 1
    held_blocks = (up, down, y * 2, y * 2 + 1)
    for n, b in enumerate(held_blocks):
        table2[n * BLK:(n + 1) * BLK, :] = table[pl.ds(pl.multiple_of(b * BLK, BLK), BLK), :]

    pl.semaphore_wait(barrier, len(near))
    trade = remote(swap.at[0], swap.at[1], sem_swap.at[0], sem_swap.at[1], partner)
    trade.start()
    trade.wait_recv()
    first = jnp.where(c == 0, kept, swap[1])
    second = jnp.where(c == 0, swap[1], kept)

    half = pl.ds(pl.multiple_of(c * HALF, HALF), HALF)

    def spot(ref, slot, px):
        return ref.at[pl.ds(pl.multiple_of((slot % NZ) * 64 + px * 16, 16), 16), half]

    def chunk_of(ref, g):
        return ref.at[pl.ds(g * CHUNK, CHUNK), half]

    tokens[pl.ds(pl.multiple_of(x * 16, 16), 16), half] = (
        jnp.concatenate([first, second], axis=0).astype(BF16)
    )

    def z_send(k, step):
        remote(
            spot(tokens, k, x), spot(tokens, k - step, x),
            sem_z_send, sem_z.at[(k - step) % NZ], at_z(step),
        ).start()

    def share(k, px):
        slot = k % NZ
        g = slot // 4
        block = spot(tokens, slot, px)
        remote(block, block, sem_c_send.at[g], sem_c.at[g], partner).start()
        remote(block, spot(tokens2, slot, px), sem_y_send.at[g], sem_y.at[g], across).start()

    def z_step(k):
        slot = k % NZ
        block = spot(tokens, slot, x)
        if k:
            remote(block, block, sem_z_send, sem_z.at[slot], partner).wait_recv()
        if k and k % REACH == 0:
            for step in range(1, REACH + 1):
                if k < 0 and step - k <= NZ // 2:
                    z_send(k, step)
                if k > 0 and step + k < NZ // 2:
                    z_send(k, -step)
        for j, xk in enumerate(XPEERS):
            seen = XPEERS.index(NX - xk)
            remote(block, block, sem_x_send.at[j], sem_x.at[seen, slot], at_x(xk)).start()
        share(k, x)

    def x_step(slot):
        for j, xk in enumerate(XPEERS):
            px = lax.rem(x + xk, NX)
            block = spot(tokens, slot, px)
            remote(block, block, sem_x_send.at[j], sem_x.at[j, slot], partner).wait_recv()
            share(slot, px)

    def rows_of(g):
        return slice(g * CHUNK, (g + 1) * CHUNK)

    word = lax.broadcasted_iota(I32, (BLK, CHUNK), 0)

    def chunk_logits(g):
        whole = chunk_of(tokens, g)
        remote(whole, whole, sem_c_send.at[g], sem_c.at[g], partner).wait_recv()
        at = rows_of(g)
        held = tokens[at, :]
        target = rows[0:1, at] - v * ROWS
        top = jnp.full((1, CHUNK), FILL, F32)
        hit_logit = jnp.zeros((1, CHUNK), F32)
        for b in range(NB):
            if b % 4 == 0:
                raw = dot(table[b * BLK:(b + 4) * BLK, :], held, ((1,), (1,)))
            score = raw[b % 4 * BLK:(b % 4 + 1) * BLK] - log_counts[0:1, b:b + 1]
            score = jnp.where(allowed[b:b + 1, at] > 0.5, score, FILL)
            logits[b * BLK:(b + 1) * BLK, at] = score
            top = jnp.maximum(top, jnp.max(score, axis=0, keepdims=True))
            hit_logit += jnp.sum(jnp.where(word + b * BLK == target, score, 0.0), axis=0, keepdims=True)
        total = jnp.zeros((1, CHUNK), F32)
        for b in range(NB):
            weight = jnp.exp(logits[b * BLK:(b + 1) * BLK, at] - top)
            logits[b * BLK:(b + 1) * BLK, at] = weight
            total += jnp.sum(weight, axis=0, keepdims=True)
        peaks[g] = top
        local = top + jnp.log(total)
        for r in range(2):
            lse_out[2 * g + r] = local[:, r * 128:(r + 1) * 128]
            tgt_out[2 * g + r] = hit_logit[:, r * 128:(r + 1) * 128]
        for i, (k, f) in enumerate(XC_PEERS):
            remote(
                lse_out.at[pl.ds(2 * g, 2)], s1.at[my_slot, pl.ds(2 * g, 2)],
                sem_s1s.at[g, i], sem_s1.at[g, my_slot], at_x(k, f),
            ).start()

    my_slot = x * 2 + c

    def slot_of(k, f):
        return lax.rem(x + k, NX) * 2 + ((1 - c) if f else c)

    far_first = sorted(range(1, NZ), key=lambda k: -min(k, NZ - k))

    def chunk_totals(g):
        two = pl.ds(2 * g, 2)
        parts = [lse_out[two]]
        for i, (k, f) in enumerate(XC_PEERS):
            there = slot_of(k, f)
            remote(
                lse_out.at[two], s1.at[there, two], sem_s1s.at[g, i], sem_s1.at[g, there], partner
            ).wait_recv()
            parts.append(s1[there, two])
        l1_out[two] = merge(parts)
        for k in far_first:
            remote(
                l1_out.at[two], s2.at[z, two], sem_s2s.at[g, k], sem_s2.at[g, z], at_z(k)
            ).start()

    peaks = [None] * 4

    for k in range(REACH, 0, -1):
        z_send(0, k)
        z_send(0, -k)
    for k in ZORDER[:9]:
        z_step(k)
    for slot in (0, 1, 15, 2, 14):
        x_step(slot)
    for k in ZORDER[9:13]:
        z_step(k)
    for slot in (3, 13, 4, 12):
        x_step(slot)
    for k in ZORDER[13:]:
        z_step(k)

    peaks2 = [None] * 4

    def pass_on(g):
        whole = chunk_of(tokens2, g)
        remote(whole, whole, sem_y_send.at[g], sem_y.at[g], partner).wait_recv()
        remote(whole, whole, sem_c2_send.at[g], sem_c2.at[g], partner).start()

    block_lane = lax.broadcasted_iota(I32, (1, NB), 1)
    block_row = lax.broadcasted_iota(I32, (NB, CHUNK), 0)

    def other_logits(g):
        whole = chunk_of(tokens2, g)
        remote(whole, whole, sem_c2_send.at[g], sem_c2.at[g], partner).wait_recv()
        at = rows_of(g)
        held = tokens2[at, :]
        may = allowed[:, at]
        top = jnp.full((1, CHUNK), FILL, F32)
        raw = dot(table2[...], held, ((1,), (1,)))
        for i, b in enumerate(held_blocks):
            less = jnp.sum(jnp.where(block_lane == b, log_counts, 0.0), axis=1, keepdims=True)
            ok = jnp.sum(jnp.where(block_row == b, may, 0.0), axis=0, keepdims=True) > 0.5
            score = jnp.where(ok, raw[i * BLK:(i + 1) * BLK] - less, FILL)
            logits2[i * BLK:(i + 1) * BLK, at] = score
            top = jnp.maximum(top, jnp.max(score, axis=0, keepdims=True))
        for i in range(4):
            logits2[i * BLK:(i + 1) * BLK, at] = jnp.exp(logits2[i * BLK:(i + 1) * BLK, at] - top)
        peaks2[g] = top

    ca, cb, cc, cd = CHUNKS
    chunk_logits(ca)
    for slot in (5, 11, 6, 10):
        x_step(slot)
    chunk_logits(cb)
    chunk_totals(ca)
    for slot in (7, 9, 8):
        x_step(slot)
    chunk_logits(cc)
    chunk_totals(cb)
    pass_on(ca)
    chunk_logits(cd)
    chunk_totals(cc)
    other_logits(ca)
    chunk_totals(cd)

    for i, (k, f) in enumerate(XC_PEERS):
        remote(tgt_out, t1.at[my_slot], sem_t1s.at[i], sem_t1.at[my_slot], at_x(k, f)).start()

    pass_on(cb)
    pass_on(cc)
    other_logits(cb)
    pass_on(cd)
    other_logits(cc)
    tsum = tgt_out[...]
    for i, (k, f) in enumerate(XC_PEERS):
        there = slot_of(k, f)
        remote(tgt_out, t1.at[there], sem_t1s.at[i], sem_t1.at[there], partner).wait_recv()
        tsum = tsum + t1[there]
    tsum_out[...] = tsum
    for k in far_first:
        remote(tsum_out.at[k // 2], t2.at[z], sem_t2s.at[k], sem_t2.at[z], at_z(k)).start()
    other_logits(cd)

    first_half = lax.broadcasted_iota(I32, (1, 128), 1) < 64
    parts = [[l1_out[r]] for r in range(8)]
    for k in far_first[::-1]:
        there = lax.rem(z + k, NZ)
        for g in CHUNKS:
            two = pl.ds(2 * g, 2)
            remote(
                l1_out.at[two], s2.at[there, two], sem_s2s.at[g, k], sem_s2.at[g, there], partner
            ).wait_recv()
        theirs = [s2[there, r] for r in range(8)]
        if k % 2:
            turned = [pltpu.roll(t, 64, 1) for t in theirs]
        for r in range(8):
            if k % 2:
                before = ((2 * r - k - 1) // 2) % 8
                parts[r].append(jnp.where(first_half, turned[before], turned[(before + 1) % 8]))
            else:
                parts[r].append(theirs[(r - k // 2) % 8])
    total_rows = [merge(p) for p in parts]
    for r in range(8):
        l_out[r] = total_rows[r]
    tell = remote(l_out, l_in, sem_l.at[0], sem_l.at[1], across)
    tell.start()

    scale = jnp.exp(jnp.concatenate(peaks, axis=1) - jnp.concatenate(total_rows, axis=1))
    deep = lax.broadcasted_iota(I32, (BLK, TOK), 0)
    own_row = rows[0:1, :] - v * ROWS
    other_row = rows[1:2, :] - v * ROWS

    def fill_probs(source, at, b, n, factor, target):
        weight = source[pl.ds(pl.multiple_of(at * BLK, BLK), BLK), :] * factor
        weight = weight - (deep + b * BLK == target).astype(F32)
        probs[n * BLK:(n + 1) * BLK, :] = weight.astype(BF16)

    for n, b in enumerate(held_blocks):
        fill_probs(logits, b, b, n, scale, own_row)
    sums[...] = dot(probs[...], tokens[...], ((1,), (0,)))

    tell.wait_recv()
    other_total = jnp.concatenate([l_in[r] for r in range(8)], axis=1)
    scale2 = jnp.exp(jnp.concatenate(peaks2, axis=1) - other_total)
    for n, to in ((0, at_y(1)), (1, at_y(3))):
        fill_probs(logits2, n, held_blocks[n], n, scale2, other_row)
        at = slice(n * BLK, (n + 1) * BLK)
        send_buf[n] = (sums[at, :] + dot(probs[at, :], tokens2[...], ((1,), (0,)))).astype(BF16)
        remote(send_buf.at[n], recv_ref.at[pl.ds(n * BLK, BLK)], sem_rs.at[n], sem_rr.at[n], to).start()
    for n in (2, 3):
        fill_probs(logits2, n, held_blocks[n], n, scale2, other_row)
    sums[2 * BLK:, :] += dot(probs[2 * BLK:, :], tokens2[...], ((1,), (0,)))
    put = pltpu.make_async_copy(sums.at[pl.ds(2 * BLK, QROWS)], own_ref, sem_out)
    put.start()

    tgt = tsum_out[0]
    for k in far_first[::-1]:
        there = lax.rem(z + k, NZ)
        remote(tsum_out.at[0], t2.at[there], sem_t2s.at[k], sem_t2.at[there], partner).wait_recv()
        theirs = t2[there]
        tgt = tgt + (pltpu.roll(theirs, 64, 1) if k % 2 else theirs)
    lane0 = x * 16 + c * 8
    loss = jnp.broadcast_to(l_out[0] - tgt, (8, 128))
    loss_ref[...] = pltpu.roll(loss, lax.rem(128 - lane0, 128), 1)

    trade.wait_send()
    tell.wait_send()
    block = tokens.at[pl.ds(0, 240), pl.ds(0, HALF)]
    remote(block, block, sem_z_send, sem_z.at[0], partner).wait_send()
    whole = chunk_of(tokens, 0)
    for j in range(3):
        remote(whole, whole, sem_x_send.at[j], sem_x.at[j, 0], partner).wait_send()
    for g in range(4):
        remote(whole, whole, sem_c_send.at[g], sem_c.at[g], partner).wait_send()
        remote(whole, whole, sem_y_send.at[g], sem_y.at[g], partner).wait_send()
        remote(whole, whole, sem_c2_send.at[g], sem_c2.at[g], partner).wait_send()
        two = pl.ds(0, 2)
        for i in range(7):
            remote(lse_out.at[two], s1.at[0, two], sem_s1s.at[g, i], sem_s1.at[g, 0], partner).wait_send()
        for k in range(1, NZ):
            remote(l1_out.at[two], s2.at[0, two], sem_s2s.at[g, k], sem_s2.at[g, 0], partner).wait_send()
    for i in range(7):
        remote(tgt_out, t1.at[0], sem_t1s.at[i], sem_t1.at[0], partner).wait_send()
    for k in range(1, NZ):
        remote(tsum_out.at[0], t2.at[0], sem_t2s.at[k], sem_t2.at[0], partner).wait_send()
    put.wait()
    for n in range(2):
        part = recv_ref.at[pl.ds(n * BLK, BLK)]
        remote(send_buf.at[n], part, sem_rs.at[n], sem_rr.at[n], partner).wait()


def body(hidden, embedding, block_counts, lang_blocks, sent_lang, targets):
    vmem, dma = pltpu.VMEM, pltpu.SemaphoreType.DMA
    anywhere = pl.BlockSpec(memory_space=pl.ANY)
    loss, own, received = pl.pallas_call(
        kernel,
        out_shape=(
            jax.ShapeDtypeStruct((8, 128), F32),
            jax.ShapeDtypeStruct((QROWS, D), F32),
            jax.ShapeDtypeStruct((QROWS, D), BF16),
        ),
        in_specs=[anywhere] * 6,
        out_specs=(pl.BlockSpec(memory_space=pltpu.VMEM), anywhere, anywhere),
        scratch_shapes=[
            vmem(hidden.shape, BF16),
            vmem((ROWS, D), BF16),
            vmem((4 * BLK, D), BF16),
            vmem((1, NB), I32),
            vmem(lang_blocks.shape[::-1], I32),
            vmem((1, 64), I32),
            vmem((32, 128), I32),
            vmem((TOK, D), BF16),
            vmem((TOK, D), BF16),
            vmem((ROWS, TOK), F32),
            vmem((4 * BLK, TOK), F32),
            vmem((4 * BLK, TOK), BF16),
            vmem((4 * BLK, D), F32),
            vmem((2, 8, HALF), F32),
            vmem((NB, TOK), F32),
            vmem((8, TOK), I32),
            vmem((8, 8, 1, 128), F32),
            vmem((NZ, 8, 1, 128), F32),
            vmem((8, 8, 1, 128), F32),
            vmem((NZ, 1, 128), F32),
            vmem((8, 1, 128), F32),
            vmem((8, 1, 128), F32),
            vmem((8, 1, 128), F32),
            vmem((8, 1, 128), F32),
            vmem((8, 1, 128), F32),
            vmem((8, 1, 128), F32),
            vmem((2, BLK, D), BF16),
            dma((6,)), dma((2,)), dma, dma((NZ,)), dma((3,)), dma((3, NZ)),
            dma((4,)), dma((4,)), dma((4,)), dma((4,)), dma((4,)), dma((4,)),
            dma((4, 7)), dma((4, 8)), dma((4, NZ)), dma((4, NZ)),
            dma((7,)), dma((8,)), dma((NZ,)), dma((NZ,)),
            dma((2,)), dma((2,)), dma((2,)), dma,
        ],
        compiler_params=pltpu.CompilerParams(
            collective_id=0, has_side_effects=True, vmem_limit_bytes=54 << 20
        ),
    )(
        hidden, embedding, block_counts.reshape(1, NB), lang_blocks.T,
        sent_lang.reshape(1, 64), targets.reshape(32, 128),
    )
    return loss[0, :8], (own + received.astype(F32)).astype(BF16)


def solution(mesh):
    in_specs = (P(("vocab", "batch"), None), P("vocab", None), P("vocab"), P(), P(), P())
    out_specs = (P(("vocab", "batch")), P(("vocab", "batch"), None))
    return jax.shard_map(body, mesh=mesh, in_specs=in_specs, out_specs=out_specs, check_vma=False)
```

```python
import functools

import jax
import jax.numpy as jnp
from jax import lax
from jax.experimental import pallas as pl
from jax.experimental.pallas import tpu as pltpu
from jax.sharding import PartitionSpec as P

MESH = pl.DeviceIdType.MESH
F32, BF16, I32 = jnp.float32, jnp.bfloat16, jnp.int32
NX, NZ, NY = 4, 16, 4
D = 1024
HALF = 512
ROWS = 1024
TOK = 1024
NB = 8
BLK = 128
QROWS = 256
CHUNK = 256
FILL = -3e38
REACH = 3
ZORDER = [0] + [s * k for k in range(1, 8) for s in (1, -1)] + [-8]
XPEERS = (1, 3, 2)
XC_PEERS = [(k, f) for f in (0, 1) for k in range(NX) if (k, f) != (0, 0)]
CHUNKS = (0, 3, 1, 2)


def remote(src, dst, send, recv, device):
    return pltpu.make_async_remote_copy(
        src_ref=src, dst_ref=dst, send_sem=send, recv_sem=recv,
        device_id=device, device_id_type=MESH,
    )


def merge(parts):
    top = functools.reduce(jnp.maximum, parts)
    total = functools.reduce(jnp.add, [jnp.exp(p - top) for p in parts])
    return top + jnp.log(total)


def dot(a, b, contract):
    return lax.dot_general(a, b, (contract, ((), ())), preferred_element_type=F32)


def kernel(
    hid_hbm, emb_hbm, counts_hbm, lists_hbm, sent_hbm, targets_hbm,
    loss_ref, own_ref, recv_ref,
    hid, table, table2, counts, lists, sent, targets,
    tokens, tokens2, logits, logits2, probs, sums, swap, allowed, rows,
    s1, s2, t1, t2, lse_out, l1_out, tgt_out, tsum_out, l_out, l_in,
    send_buf,
    sem_load, sem_swap, sem_z_send, sem_z, sem_x_send, sem_x, sem_c_send, sem_c,
    sem_y_send, sem_y, sem_c2_send, sem_c2,
    sem_s1s, sem_s1, sem_s2s, sem_s2, sem_t1s, sem_t1, sem_t2s, sem_t2,
    sem_l, sem_rs, sem_rr, sem_out,
):
    v, y = lax.axis_index("vocab"), lax.axis_index("batch")
    c = lax.rem(v, 2)
    z = lax.rem(lax.div(v, 2), NZ)
    x = lax.div(v, 2 * NZ)

    def dev(px, pz, pc, py):
        return {"vocab": (px * NZ + pz) * 2 + pc, "batch": py}

    def at_z(k):
        return dev(x, lax.rem(z + k + 2 * NZ, NZ), c, y)

    def at_x(k, flip=0):
        return dev(lax.rem(x + k, NX), z, (1 - c) if flip else c, y)

    def at_y(k):
        return dev(x, z, c, lax.rem(y + k, NY))

    partner = dev(x, z, 1 - c, y)
    across = at_y(2)

    pairs = (
        (hid_hbm, hid), (lists_hbm, lists), (sent_hbm, sent), (targets_hbm, targets),
        (counts_hbm, counts), (emb_hbm, table),
    )
    loads = [
        pltpu.make_async_copy(src, dst, sem_load.at[i]) for i, (src, dst) in enumerate(pairs)
    ]
    for load in loads:
        load.start()

    barrier = pltpu.get_barrier_semaphore()
    near = [at_x(k, f) for k, f in XC_PEERS]
    near += [at_z(s * k) for k in range(1, REACH + 1) for s in (1, -1)]
    near += [at_y(k) for k in range(1, NY)]
    for peer in near:
        pl.semaphore_signal(barrier, inc=1, device_id=peer, device_id_type=MESH)

    loads[0].wait()
    mine = hid[...].astype(F32)
    low, high = mine[:, :HALF], mine[:, HALF:]
    swap[0] = jnp.where(c == 0, high, low)
    kept = jnp.where(c == 0, low, high)
    for load in loads[1:4]:
        load.wait()
    lane = lax.broadcasted_iota(I32, (1, TOK), 1)
    lane_x, lane_z = (lane >> 4) & 3, (z + (lane >> 6)) & (NZ - 1)
    place = ((lane_z & 1) << 6) + (((lane >> 3) & 1) << 5) + (lane & 7)
    ids = targets[...]
    digits = jnp.concatenate([ids & 255, (ids >> 8) & 255, ids >> 16], axis=0).astype(F32).astype(BF16)
    here = lax.broadcasted_iota(I32, (32, TOK), 0) == lane_x * 8 + (lane_z >> 1)

    def plane_targets(py):
        pick = lax.broadcasted_iota(I32, (128, TOK), 0) == place + py * 8
        found = dot(digits, pick.astype(F32).astype(BF16), ((1,), (0,)))
        value = found[:32] + found[32:64] * 256.0 + found[64:] * 65536.0
        return jnp.sum(jnp.where(here, value, 0.0), axis=0, keepdims=True).astype(I32)

    own_targets = plane_targets(y)
    other_targets = plane_targets(lax.rem(y + 2, NY))
    rows[0:1, :] = own_targets
    rows[1:2, :] = other_targets
    sentence = lax.broadcasted_iota(I32, (64, TOK), 0) == lane_x * NZ + lane_z
    lang = dot(
        jnp.broadcast_to(sent[...], (8, 64)).astype(F32).astype(BF16),
        sentence.astype(F32).astype(BF16), ((1,), (0,)),
    )[0:1].astype(I32)
    lists_now = lists[...]
    member = jnp.concatenate(
        [jnp.any(lists_now == v * NB + b, axis=0, keepdims=True).astype(F32) for b in range(NB)],
        axis=0,
    )
    hit = (lax.broadcasted_iota(I32, (lists.shape[1], TOK), 0) == lang).astype(F32)
    allowed[...] = dot(member, hit, ((1,), (0,)))
    loads[4].wait()
    loads[5].wait()
    log_counts = jnp.log(counts[...].astype(F32))
    up = lax.rem(y + 1, NY) * 2
    down = lax.rem(y + 3, NY) * 2 + 1
    held_blocks = (up, down, y * 2, y * 2 + 1)
    for n, b in enumerate(held_blocks):
        table2[n * BLK:(n + 1) * BLK, :] = table[pl.ds(pl.multiple_of(b * BLK, BLK), BLK), :]

    pl.semaphore_wait(barrier, len(near))
    trade = remote(swap.at[0], swap.at[1], sem_swap.at[0], sem_swap.at[1], partner)
    trade.start()
    trade.wait_recv()
    first = jnp.where(c == 0, kept, swap[1])
    second = jnp.where(c == 0, swap[1], kept)

    half = pl.ds(pl.multiple_of(c * HALF, HALF), HALF)

    def spot(ref, slot, px):
        return ref.at[pl.ds(pl.multiple_of((slot % NZ) * 64 + px * 16, 16), 16), half]

    def chunk_of(ref, g):
        return ref.at[pl.ds(g * CHUNK, CHUNK), half]

    tokens[pl.ds(pl.multiple_of(x * 16, 16), 16), half] = (
        jnp.concatenate([first, second], axis=0).astype(BF16)
    )

    def z_send(k, step):
        remote(
            spot(tokens, k, x), spot(tokens, k - step, x),
            sem_z_send, sem_z.at[(k - step) % NZ], at_z(step),
        ).start()

    def share(k, px):
        slot = k % NZ
        g = slot // 4
        block = spot(tokens, slot, px)
        remote(block, block, sem_c_send.at[g], sem_c.at[g], partner).start()
        remote(block, spot(tokens2, slot, px), sem_y_send.at[g], sem_y.at[g], across).start()

    def z_step(k):
        slot = k % NZ
        block = spot(tokens, slot, x)
        if k:
            remote(block, block, sem_z_send, sem_z.at[slot], partner).wait_recv()
        if k and k % REACH == 0:
            for step in range(1, REACH + 1):
                if k < 0 and step - k <= NZ // 2:
                    z_send(k, step)
                if k > 0 and step + k < NZ // 2:
                    z_send(k, -step)
        for j, xk in enumerate(XPEERS):
            seen = XPEERS.index(NX - xk)
            remote(block, block, sem_x_send.at[j], sem_x.at[seen, slot], at_x(xk)).start()
        share(k, x)

    def x_step(slot):
        for j, xk in enumerate(XPEERS):
            px = lax.rem(x + xk, NX)
            block = spot(tokens, slot, px)
            remote(block, block, sem_x_send.at[j], sem_x.at[j, slot], partner).wait_recv()
            share(slot, px)

    def rows_of(g):
        return slice(g * CHUNK, (g + 1) * CHUNK)

    word = lax.broadcasted_iota(I32, (BLK, CHUNK), 0)

    def chunk_logits(g):
        whole = chunk_of(tokens, g)
        remote(whole, whole, sem_c_send.at[g], sem_c.at[g], partner).wait_recv()
        at = rows_of(g)
        held = tokens[at, :]
        target = rows[0:1, at] - v * ROWS
        top = jnp.full((1, CHUNK), FILL, F32)
        hit_logit = jnp.zeros((1, CHUNK), F32)
        for b in range(NB):
            if b % 4 == 0:
                raw = dot(table[b * BLK:(b + 4) * BLK, :], held, ((1,), (1,)))
            score = raw[b % 4 * BLK:(b % 4 + 1) * BLK] - log_counts[0:1, b:b + 1]
            score = jnp.where(allowed[b:b + 1, at] > 0.5, score, FILL)
            logits[b * BLK:(b + 1) * BLK, at] = score
            top = jnp.maximum(top, jnp.max(score, axis=0, keepdims=True))
            hit_logit += jnp.sum(jnp.where(word + b * BLK == target, score, 0.0), axis=0, keepdims=True)
        total = jnp.zeros((1, CHUNK), F32)
        for b in range(NB):
            weight = jnp.exp(logits[b * BLK:(b + 1) * BLK, at] - top)
            logits[b * BLK:(b + 1) * BLK, at] = weight
            total += jnp.sum(weight, axis=0, keepdims=True)
        peaks[g] = top
        local = top + jnp.log(total)
        for r in range(2):
            lse_out[2 * g + r] = local[:, r * 128:(r + 1) * 128]
            tgt_out[2 * g + r] = hit_logit[:, r * 128:(r + 1) * 128]
        for i, (k, f) in enumerate(XC_PEERS):
            remote(
                lse_out.at[pl.ds(2 * g, 2)], s1.at[my_slot, pl.ds(2 * g, 2)],
                sem_s1s.at[g, i], sem_s1.at[g, my_slot], at_x(k, f),
            ).start()

    my_slot = x * 2 + c

    def slot_of(k, f):
        return lax.rem(x + k, NX) * 2 + ((1 - c) if f else c)

    far_first = sorted(range(1, NZ), key=lambda k: -min(k, NZ - k))

    def chunk_totals(g):
        two = pl.ds(2 * g, 2)
        parts = [lse_out[two]]
        for i, (k, f) in enumerate(XC_PEERS):
            there = slot_of(k, f)
            remote(
                lse_out.at[two], s1.at[there, two], sem_s1s.at[g, i], sem_s1.at[g, there], partner
            ).wait_recv()
            parts.append(s1[there, two])
        l1_out[two] = merge(parts)
        for k in far_first:
            remote(
                l1_out.at[two], s2.at[z, two], sem_s2s.at[g, k], sem_s2.at[g, z], at_z(k)
            ).start()

    peaks = [None] * 4

    for k in range(REACH, 0, -1):
        z_send(0, k)
        z_send(0, -k)
    for k in ZORDER[:7]:
        z_step(k)
    for slot in (0, 1, 15, 2, 14):
        x_step(slot)
    for k in ZORDER[7:13]:
        z_step(k)
    for slot in (3, 13, 4, 12):
        x_step(slot)
    for k in ZORDER[13:]:
        z_step(k)

    peaks2 = [None] * 4

    def pass_on(g):
        whole = chunk_of(tokens2, g)
        remote(whole, whole, sem_y_send.at[g], sem_y.at[g], partner).wait_recv()
        remote(whole, whole, sem_c2_send.at[g], sem_c2.at[g], partner).start()

    block_lane = lax.broadcasted_iota(I32, (1, NB), 1)
    block_row = lax.broadcasted_iota(I32, (NB, CHUNK), 0)

    def other_logits(g):
        whole = chunk_of(tokens2, g)
        remote(whole, whole, sem_c2_send.at[g], sem_c2.at[g], partner).wait_recv()
        at = rows_of(g)
        held = tokens2[at, :]
        may = allowed[:, at]
        top = jnp.full((1, CHUNK), FILL, F32)
        raw = dot(table2[...], held, ((1,), (1,)))
        for i, b in enumerate(held_blocks):
            less = jnp.sum(jnp.where(block_lane == b, log_counts, 0.0), axis=1, keepdims=True)
            ok = jnp.sum(jnp.where(block_row == b, may, 0.0), axis=0, keepdims=True) > 0.5
            score = jnp.where(ok, raw[i * BLK:(i + 1) * BLK] - less, FILL)
            logits2[i * BLK:(i + 1) * BLK, at] = score
            top = jnp.maximum(top, jnp.max(score, axis=0, keepdims=True))
        for i in range(4):
            logits2[i * BLK:(i + 1) * BLK, at] = jnp.exp(logits2[i * BLK:(i + 1) * BLK, at] - top)
        peaks2[g] = top

    ca, cb, cc, cd = CHUNKS
    chunk_logits(ca)
    for slot in (5, 11, 6, 10):
        x_step(slot)
    chunk_logits(cb)
    chunk_totals(ca)
    for slot in (7, 9, 8):
        x_step(slot)
    chunk_logits(cc)
    chunk_totals(cb)
    pass_on(ca)
    chunk_logits(cd)
    chunk_totals(cc)
    other_logits(ca)
    chunk_totals(cd)

    for i, (k, f) in enumerate(XC_PEERS):
        remote(tgt_out, t1.at[my_slot], sem_t1s.at[i], sem_t1.at[my_slot], at_x(k, f)).start()

    pass_on(cb)
    pass_on(cc)
    other_logits(cb)
    pass_on(cd)
    other_logits(cc)
    tsum = tgt_out[...]
    for i, (k, f) in enumerate(XC_PEERS):
        there = slot_of(k, f)
        remote(tgt_out, t1.at[there], sem_t1s.at[i], sem_t1.at[there], partner).wait_recv()
        tsum = tsum + t1[there]
    tsum_out[...] = tsum
    for k in far_first:
        remote(tsum_out.at[k // 2], t2.at[z], sem_t2s.at[k], sem_t2.at[z], at_z(k)).start()
    other_logits(cd)

    first_half = lax.broadcasted_iota(I32, (1, 128), 1) < 64
    parts = [[l1_out[r]] for r in range(8)]
    for k in far_first[::-1]:
        there = lax.rem(z + k, NZ)
        for g in CHUNKS:
            two = pl.ds(2 * g, 2)
            remote(
                l1_out.at[two], s2.at[there, two], sem_s2s.at[g, k], sem_s2.at[g, there], partner
            ).wait_recv()
        theirs = [s2[there, r] for r in range(8)]
        if k % 2:
            turned = [pltpu.roll(t, 64, 1) for t in theirs]
        for r in range(8):
            if k % 2:
                before = ((2 * r - k - 1) // 2) % 8
                parts[r].append(jnp.where(first_half, turned[before], turned[(before + 1) % 8]))
            else:
                parts[r].append(theirs[(r - k // 2) % 8])
    total_rows = [merge(p) for p in parts]
    for r in range(8):
        l_out[r] = total_rows[r]
    tell = remote(l_out, l_in, sem_l.at[0], sem_l.at[1], across)
    tell.start()

    scale = jnp.exp(jnp.concatenate(peaks, axis=1) - jnp.concatenate(total_rows, axis=1))
    deep = lax.broadcasted_iota(I32, (BLK, TOK), 0)
    own_row = rows[0:1, :] - v * ROWS
    other_row = rows[1:2, :] - v * ROWS

    def fill_probs(source, at, b, n, factor, target):
        weight = source[pl.ds(pl.multiple_of(at * BLK, BLK), BLK), :] * factor
        weight = weight - (deep + b * BLK == target).astype(F32)
        probs[n * BLK:(n + 1) * BLK, :] = weight.astype(BF16)

    for n, b in enumerate(held_blocks):
        fill_probs(logits, b, b, n, scale, own_row)
    sums[...] = dot(probs[...], tokens[...], ((1,), (0,)))

    tell.wait_recv()
    other_total = jnp.concatenate([l_in[r] for r in range(8)], axis=1)
    scale2 = jnp.exp(jnp.concatenate(peaks2, axis=1) - other_total)
    for n, to in ((0, at_y(1)), (1, at_y(3))):
        fill_probs(logits2, n, held_blocks[n], n, scale2, other_row)
        at = slice(n * BLK, (n + 1) * BLK)
        send_buf[n] = (sums[at, :] + dot(probs[at, :], tokens2[...], ((1,), (0,)))).astype(BF16)
        remote(send_buf.at[n], recv_ref.at[pl.ds(n * BLK, BLK)], sem_rs.at[n], sem_rr.at[n], to).start()
    for n in (2, 3):
        fill_probs(logits2, n, held_blocks[n], n, scale2, other_row)
    sums[2 * BLK:, :] += dot(probs[2 * BLK:, :], tokens2[...], ((1,), (0,)))
    put = pltpu.make_async_copy(sums.at[pl.ds(2 * BLK, QROWS)], own_ref, sem_out)
    put.start()

    tgt = tsum_out[0]
    for k in far_first[::-1]:
        there = lax.rem(z + k, NZ)
        remote(tsum_out.at[0], t2.at[there], sem_t2s.at[k], sem_t2.at[there], partner).wait_recv()
        theirs = t2[there]
        tgt = tgt + (pltpu.roll(theirs, 64, 1) if k % 2 else theirs)
    lane0 = x * 16 + c * 8
    loss = jnp.broadcast_to(l_out[0] - tgt, (8, 128))
    loss_ref[...] = pltpu.roll(loss, lax.rem(128 - lane0, 128), 1)

    trade.wait_send()
    tell.wait_send()
    block = tokens.at[pl.ds(0, 240), pl.ds(0, HALF)]
    remote(block, block, sem_z_send, sem_z.at[0], partner).wait_send()
    whole = chunk_of(tokens, 0)
    for j in range(3):
        remote(whole, whole, sem_x_send.at[j], sem_x.at[j, 0], partner).wait_send()
    for g in range(4):
        remote(whole, whole, sem_c_send.at[g], sem_c.at[g], partner).wait_send()
        remote(whole, whole, sem_y_send.at[g], sem_y.at[g], partner).wait_send()
        remote(whole, whole, sem_c2_send.at[g], sem_c2.at[g], partner).wait_send()
        two = pl.ds(0, 2)
        for i in range(7):
            remote(lse_out.at[two], s1.at[0, two], sem_s1s.at[g, i], sem_s1.at[g, 0], partner).wait_send()
        for k in range(1, NZ):
            remote(l1_out.at[two], s2.at[0, two], sem_s2s.at[g, k], sem_s2.at[g, 0], partner).wait_send()
    for i in range(7):
        remote(tgt_out, t1.at[0], sem_t1s.at[i], sem_t1.at[0], partner).wait_send()
    for k in range(1, NZ):
        remote(tsum_out.at[0], t2.at[0], sem_t2s.at[k], sem_t2.at[0], partner).wait_send()
    put.wait()
    for n in range(2):
        part = recv_ref.at[pl.ds(n * BLK, BLK)]
        remote(send_buf.at[n], part, sem_rs.at[n], sem_rr.at[n], partner).wait()


def body(hidden, embedding, block_counts, lang_blocks, sent_lang, targets):
    vmem, dma = pltpu.VMEM, pltpu.SemaphoreType.DMA
    anywhere = pl.BlockSpec(memory_space=pl.ANY)
    loss, own, received = pl.pallas_call(
        kernel,
        out_shape=(
            jax.ShapeDtypeStruct((8, 128), F32),
            jax.ShapeDtypeStruct((QROWS, D), F32),
            jax.ShapeDtypeStruct((QROWS, D), BF16),
        ),
        in_specs=[anywhere] * 6,
        out_specs=(pl.BlockSpec(memory_space=pltpu.VMEM), anywhere, anywhere),
        scratch_shapes=[
            vmem(hidden.shape, BF16),
            vmem((ROWS, D), BF16),
            vmem((4 * BLK, D), BF16),
            vmem((1, NB), I32),
            vmem(lang_blocks.shape[::-1], I32),
            vmem((1, 64), I32),
            vmem((32, 128), I32),
            vmem((TOK, D), BF16),
            vmem((TOK, D), BF16),
            vmem((ROWS, TOK), F32),
            vmem((4 * BLK, TOK), F32),
            vmem((4 * BLK, TOK), BF16),
            vmem((4 * BLK, D), F32),
            vmem((2, 8, HALF), F32),
            vmem((NB, TOK), F32),
            vmem((8, TOK), I32),
            vmem((8, 8, 1, 128), F32),
            vmem((NZ, 8, 1, 128), F32),
            vmem((8, 8, 1, 128), F32),
            vmem((NZ, 1, 128), F32),
            vmem((8, 1, 128), F32),
            vmem((8, 1, 128), F32),
            vmem((8, 1, 128), F32),
            vmem((8, 1, 128), F32),
            vmem((8, 1, 128), F32),
            vmem((8, 1, 128), F32),
            vmem((2, BLK, D), BF16),
            dma((6,)), dma((2,)), dma, dma((NZ,)), dma((3,)), dma((3, NZ)),
            dma((4,)), dma((4,)), dma((4,)), dma((4,)), dma((4,)), dma((4,)),
            dma((4, 7)), dma((4, 8)), dma((4, NZ)), dma((4, NZ)),
            dma((7,)), dma((8,)), dma((NZ,)), dma((NZ,)),
            dma((2,)), dma((2,)), dma((2,)), dma,
        ],
        compiler_params=pltpu.CompilerParams(
            collective_id=0, has_side_effects=True, vmem_limit_bytes=54 << 20
        ),
    )(
        hidden, embedding, block_counts.reshape(1, NB), lang_blocks.T,
        sent_lang.reshape(1, 64), targets.reshape(32, 128),
    )
    return loss[0, :8], (own + received.astype(F32)).astype(BF16)


def solution(mesh):
    in_specs = (P(("vocab", "batch"), None), P("vocab", None), P("vocab"), P(), P(), P())
    out_specs = (P(("vocab", "batch")), P(("vocab", "batch"), None))
    return jax.shard_map(body, mesh=mesh, in_specs=in_specs, out_specs=out_specs, check_vma=False)
```

```python
import functools

import jax
import jax.numpy as jnp
from jax import lax
from jax.experimental import pallas as pl
from jax.experimental.pallas import tpu as pltpu
from jax.sharding import PartitionSpec as P

MESH = pl.DeviceIdType.MESH
F32, BF16, I32 = jnp.float32, jnp.bfloat16, jnp.int32
NX, NZ, NY = 4, 16, 4
D = 1024
HALF = 512
ROWS = 1024
TOK = 1024
NB = 8
BLK = 128
QROWS = 256
CHUNK = 256
FILL = -3e38
REACH = 3
ZORDER = [0] + [s * k for k in range(1, 8) for s in (1, -1)] + [-8]
XPEERS = (1, 3, 2)
XC_PEERS = [(k, f) for f in (0, 1) for k in range(NX) if (k, f) != (0, 0)]
CHUNKS = (0, 3, 1, 2)


def remote(src, dst, send, recv, device):
    return pltpu.make_async_remote_copy(
        src_ref=src, dst_ref=dst, send_sem=send, recv_sem=recv,
        device_id=device, device_id_type=MESH,
    )


def merge(parts):
    top = functools.reduce(jnp.maximum, parts)
    total = functools.reduce(jnp.add, [jnp.exp(p - top) for p in parts])
    return top + jnp.log(total)


def dot(a, b, contract):
    return lax.dot_general(a, b, (contract, ((), ())), preferred_element_type=F32)


def kernel(
    hid_hbm, emb_hbm, counts_hbm, lists_hbm, sent_hbm, targets_hbm,
    loss_ref, own_ref, recv_ref,
    hid, table, table2, counts, lists, sent, targets,
    tokens, tokens2, logits, logits2, probs, sums, swap, allowed, rows,
    s1, s2, t1, t2, lse_out, l1_out, tgt_out, tsum_out, l_out, l_in,
    send_buf,
    sem_load, sem_swap, sem_z_send, sem_z, sem_x_send, sem_x, sem_c_send, sem_c,
    sem_y_send, sem_y, sem_c2_send, sem_c2,
    sem_s1s, sem_s1, sem_s2s, sem_s2, sem_t1s, sem_t1, sem_t2s, sem_t2,
    sem_l, sem_rs, sem_rr, sem_out,
):
    v, y = lax.axis_index("vocab"), lax.axis_index("batch")
    c = lax.rem(v, 2)
    z = lax.rem(lax.div(v, 2), NZ)
    x = lax.div(v, 2 * NZ)

    def dev(px, pz, pc, py):
        return {"vocab": (px * NZ + pz) * 2 + pc, "batch": py}

    def at_z(k):
        return dev(x, lax.rem(z + k + 2 * NZ, NZ), c, y)

    def at_x(k, flip=0):
        return dev(lax.rem(x + k, NX), z, (1 - c) if flip else c, y)

    def at_y(k):
        return dev(x, z, c, lax.rem(y + k, NY))

    partner = dev(x, z, 1 - c, y)
    across = at_y(2)

    pairs = (
        (hid_hbm, hid), (lists_hbm, lists), (sent_hbm, sent), (targets_hbm, targets),
        (counts_hbm, counts), (emb_hbm, table),
    )
    loads = [
        pltpu.make_async_copy(src, dst, sem_load.at[i]) for i, (src, dst) in enumerate(pairs)
    ]
    for load in loads:
        load.start()

    barrier = pltpu.get_barrier_semaphore()
    near = [at_x(k, f) for k, f in XC_PEERS]
    near += [at_z(s * k) for k in range(1, REACH + 1) for s in (1, -1)]
    near += [at_y(k) for k in range(1, NY)]
    for peer in near:
        pl.semaphore_signal(barrier, inc=1, device_id=peer, device_id_type=MESH)

    loads[0].wait()
    mine = hid[...].astype(F32)
    low, high = mine[:, :HALF], mine[:, HALF:]
    swap[0] = jnp.where(c == 0, high, low)
    kept = jnp.where(c == 0, low, high)
    for load in loads[1:4]:
        load.wait()
    lane = lax.broadcasted_iota(I32, (1, TOK), 1)
    lane_x, lane_z = (lane >> 4) & 3, (z + (lane >> 6)) & (NZ - 1)
    place = ((lane_z & 1) << 6) + (((lane >> 3) & 1) << 5) + (lane & 7)
    ids = targets[...]
    digits = jnp.concatenate([ids & 255, (ids >> 8) & 255, ids >> 16], axis=0).astype(F32).astype(BF16)
    here = lax.broadcasted_iota(I32, (32, TOK), 0) == lane_x * 8 + (lane_z >> 1)

    def plane_targets(py):
        pick = lax.broadcasted_iota(I32, (128, TOK), 0) == place + py * 8
        found = dot(digits, pick.astype(F32).astype(BF16), ((1,), (0,)))
        value = found[:32] + found[32:64] * 256.0 + found[64:] * 65536.0
        return jnp.sum(jnp.where(here, value, 0.0), axis=0, keepdims=True).astype(I32)

    own_targets = plane_targets(y)
    other_targets = plane_targets(lax.rem(y + 2, NY))
    rows[0:1, :] = own_targets
    rows[1:2, :] = other_targets
    sentence = lax.broadcasted_iota(I32, (64, TOK), 0) == lane_x * NZ + lane_z
    lang = dot(
        jnp.broadcast_to(sent[...], (8, 64)).astype(F32).astype(BF16),
        sentence.astype(F32).astype(BF16), ((1,), (0,)),
    )[0:1].astype(I32)
    lists_now = lists[...]
    member = jnp.concatenate(
        [jnp.any(lists_now == v * NB + b, axis=0, keepdims=True).astype(F32) for b in range(NB)],
        axis=0,
    )
    hit = (lax.broadcasted_iota(I32, (lists.shape[1], TOK), 0) == lang).astype(F32)
    allowed[...] = dot(member, hit, ((1,), (0,)))
    loads[4].wait()
    loads[5].wait()
    log_counts = jnp.log(counts[...].astype(F32))
    up = lax.rem(y + 1, NY) * 2
    down = lax.rem(y + 3, NY) * 2 + 1
    held_blocks = (up, down, y * 2, y * 2 + 1)
    for n, b in enumerate(held_blocks):
        table2[n * BLK:(n + 1) * BLK, :] = table[pl.ds(pl.multiple_of(b * BLK, BLK), BLK), :]

    pl.semaphore_wait(barrier, len(near))
    trade = remote(swap.at[0], swap.at[1], sem_swap.at[0], sem_swap.at[1], partner)
    trade.start()
    trade.wait_recv()
    first = jnp.where(c == 0, kept, swap[1])
    second = jnp.where(c == 0, swap[1], kept)

    half = pl.ds(pl.multiple_of(c * HALF, HALF), HALF)

    def spot(ref, slot, px):
        return ref.at[pl.ds(pl.multiple_of((slot % NZ) * 64 + px * 16, 16), 16), half]

    def chunk_of(ref, g):
        return ref.at[pl.ds(g * CHUNK, CHUNK), half]

    tokens[pl.ds(pl.multiple_of(x * 16, 16), 16), half] = (
        jnp.concatenate([first, second], axis=0).astype(BF16)
    )

    def z_send(k, step):
        remote(
            spot(tokens, k, x), spot(tokens, k - step, x),
            sem_z_send, sem_z.at[(k - step) % NZ], at_z(step),
        ).start()

    def share(k, px):
        slot = k % NZ
        g = slot // 4
        block = spot(tokens, slot, px)
        remote(block, block, sem_c_send.at[g], sem_c.at[g], partner).start()
        remote(block, spot(tokens2, slot, px), sem_y_send.at[g], sem_y.at[g], across).start()

    def z_step(k):
        slot = k % NZ
        block = spot(tokens, slot, x)
        if k:
            remote(block, block, sem_z_send, sem_z.at[slot], partner).wait_recv()
        if k and k % REACH == 0:
            for step in range(1, REACH + 1):
                if k < 0 and step - k <= NZ // 2:
                    z_send(k, step)
                if k > 0 and step + k < NZ // 2:
                    z_send(k, -step)
        for j, xk in enumerate(XPEERS):
            seen = XPEERS.index(NX - xk)
            remote(block, block, sem_x_send.at[j], sem_x.at[seen, slot], at_x(xk)).start()
        share(k, x)

    def x_step(slot):
        for j, xk in enumerate(XPEERS):
            px = lax.rem(x + xk, NX)
            block = spot(tokens, slot, px)
            remote(block, block, sem_x_send.at[j], sem_x.at[j, slot], partner).wait_recv()
            share(slot, px)

    def rows_of(g):
        return slice(g * CHUNK, (g + 1) * CHUNK)

    word = lax.broadcasted_iota(I32, (BLK, CHUNK), 0)

    def chunk_logits(g):
        whole = chunk_of(tokens, g)
        remote(whole, whole, sem_c_send.at[g], sem_c.at[g], partner).wait_recv()
        at = rows_of(g)
        held = tokens[at, :]
        target = rows[0:1, at] - v * ROWS
        top = jnp.full((1, CHUNK), FILL, F32)
        hit_logit = jnp.zeros((1, CHUNK), F32)
        for b in range(NB):
            if b % 4 == 0:
                raw = dot(table[b * BLK:(b + 4) * BLK, :], held, ((1,), (1,)))
            score = raw[b % 4 * BLK:(b % 4 + 1) * BLK] - log_counts[0:1, b:b + 1]
            score = jnp.where(allowed[b:b + 1, at] > 0.5, score, FILL)
            logits[b * BLK:(b + 1) * BLK, at] = score
            top = jnp.maximum(top, jnp.max(score, axis=0, keepdims=True))
            hit_logit += jnp.sum(jnp.where(word + b * BLK == target, score, 0.0), axis=0, keepdims=True)
        total = jnp.zeros((1, CHUNK), F32)
        for b in range(NB):
            weight = jnp.exp(logits[b * BLK:(b + 1) * BLK, at] - top)
            logits[b * BLK:(b + 1) * BLK, at] = weight
            total += jnp.sum(weight, axis=0, keepdims=True)
        peaks[g] = top
        local = top + jnp.log(total)
        for r in range(2):
            lse_out[2 * g + r] = local[:, r * 128:(r + 1) * 128]
            tgt_out[2 * g + r] = hit_logit[:, r * 128:(r + 1) * 128]
        for i, (k, f) in enumerate(XC_PEERS):
            remote(
                lse_out.at[pl.ds(2 * g, 2)], s1.at[my_slot, pl.ds(2 * g, 2)],
                sem_s1s.at[g, i], sem_s1.at[g, my_slot], at_x(k, f),
            ).start()

    my_slot = x * 2 + c

    def slot_of(k, f):
        return lax.rem(x + k, NX) * 2 + ((1 - c) if f else c)

    far_first = sorted(range(1, NZ), key=lambda k: -min(k, NZ - k))

    def chunk_totals(g):
        two = pl.ds(2 * g, 2)
        parts = [lse_out[two]]
        for i, (k, f) in enumerate(XC_PEERS):
            there = slot_of(k, f)
            remote(
                lse_out.at[two], s1.at[there, two], sem_s1s.at[g, i], sem_s1.at[g, there], partner
            ).wait_recv()
            parts.append(s1[there, two])
        l1_out[two] = merge(parts)
        for k in far_first:
            remote(
                l1_out.at[two], s2.at[z, two], sem_s2s.at[g, k], sem_s2.at[g, z], at_z(k)
            ).start()

    peaks = [None] * 4

    for k in range(REACH, 0, -1):
        z_send(0, k)
        z_send(0, -k)
    for k in ZORDER[:7]:
        z_step(k)
    for slot in (0, 1, 15, 2, 14):
        x_step(slot)
    for k in ZORDER[7:13]:
        z_step(k)
    for slot in (3, 13, 4, 12):
        x_step(slot)
    for k in ZORDER[13:]:
        z_step(k)

    peaks2 = [None] * 4

    def pass_on(g):
        whole = chunk_of(tokens2, g)
        remote(whole, whole, sem_y_send.at[g], sem_y.at[g], partner).wait_recv()
        remote(whole, whole, sem_c2_send.at[g], sem_c2.at[g], partner).start()

    block_lane = lax.broadcasted_iota(I32, (1, NB), 1)
    block_row = lax.broadcasted_iota(I32, (NB, CHUNK), 0)

    def other_logits(g):
        whole = chunk_of(tokens2, g)
        remote(whole, whole, sem_c2_send.at[g], sem_c2.at[g], partner).wait_recv()
        at = rows_of(g)
        held = tokens2[at, :]
        may = allowed[:, at]
        top = jnp.full((1, CHUNK), FILL, F32)
        raw = dot(table2[...], held, ((1,), (1,)))
        for i, b in enumerate(held_blocks):
            less = jnp.sum(jnp.where(block_lane == b, log_counts, 0.0), axis=1, keepdims=True)
            ok = jnp.sum(jnp.where(block_row == b, may, 0.0), axis=0, keepdims=True) > 0.5
            score = jnp.where(ok, raw[i * BLK:(i + 1) * BLK] - less, FILL)
            logits2[i * BLK:(i + 1) * BLK, at] = score
            top = jnp.maximum(top, jnp.max(score, axis=0, keepdims=True))
        for i in range(4):
            logits2[i * BLK:(i + 1) * BLK, at] = jnp.exp(logits2[i * BLK:(i + 1) * BLK, at] - top)
        peaks2[g] = top

    ca, cb, cc, cd = CHUNKS
    chunk_logits(ca)
    for slot in (5, 11, 6, 10):
        x_step(slot)
    chunk_logits(cb)
    chunk_totals(ca)
    for slot in (7, 9, 8):
        x_step(slot)
    chunk_logits(cc)
    chunk_totals(cb)
    pass_on(ca)
    chunk_logits(cd)
    chunk_totals(cc)
    other_logits(ca)
    chunk_totals(cd)

    pass_on(cb)
    pass_on(cc)
    other_logits(cb)
    pass_on(cd)
    other_logits(cc)
    other_logits(cd)

    first_half = lax.broadcasted_iota(I32, (1, 128), 1) < 64
    parts = [[l1_out[r]] for r in range(8)]
    for k in far_first[::-1]:
        there = lax.rem(z + k, NZ)
        for g in CHUNKS:
            two = pl.ds(2 * g, 2)
            remote(
                l1_out.at[two], s2.at[there, two], sem_s2s.at[g, k], sem_s2.at[g, there], partner
            ).wait_recv()
        theirs = [s2[there, r] for r in range(8)]
        if k % 2:
            turned = [pltpu.roll(t, 64, 1) for t in theirs]
        for r in range(8):
            if k % 2:
                before = ((2 * r - k - 1) // 2) % 8
                parts[r].append(jnp.where(first_half, turned[before], turned[(before + 1) % 8]))
            else:
                parts[r].append(theirs[(r - k // 2) % 8])
    total_rows = [merge(p) for p in parts]
    for r in range(8):
        l_out[r] = total_rows[r]
    tell = remote(l_out, l_in, sem_l.at[0], sem_l.at[1], across)
    tell.start()
    for i, (k, f) in enumerate(XC_PEERS):
        remote(tgt_out, t1.at[my_slot], sem_t1s.at[i], sem_t1.at[my_slot], at_x(k, f)).start()

    scale = jnp.exp(jnp.concatenate(peaks, axis=1) - jnp.concatenate(total_rows, axis=1))
    deep = lax.broadcasted_iota(I32, (BLK, TOK), 0)
    own_row = rows[0:1, :] - v * ROWS
    other_row = rows[1:2, :] - v * ROWS

    def fill_probs(source, at, b, n, factor, target):
        weight = source[pl.ds(pl.multiple_of(at * BLK, BLK), BLK), :] * factor
        weight = weight - (deep + b * BLK == target).astype(F32)
        probs[n * BLK:(n + 1) * BLK, :] = weight.astype(BF16)

    for n, b in enumerate(held_blocks):
        fill_probs(logits, b, b, n, scale, own_row)
    sums[...] = dot(probs[...], tokens[...], ((1,), (0,)))

    tell.wait_recv()
    other_total = jnp.concatenate([l_in[r] for r in range(8)], axis=1)
    scale2 = jnp.exp(jnp.concatenate(peaks2, axis=1) - other_total)
    for n, to in ((0, at_y(1)), (1, at_y(3))):
        fill_probs(logits2, n, held_blocks[n], n, scale2, other_row)
        at = slice(n * BLK, (n + 1) * BLK)
        send_buf[n] = (sums[at, :] + dot(probs[at, :], tokens2[...], ((1,), (0,)))).astype(BF16)
        remote(send_buf.at[n], recv_ref.at[pl.ds(n * BLK, BLK)], sem_rs.at[n], sem_rr.at[n], to).start()
    tsum = tgt_out[...]
    for i, (k, f) in enumerate(XC_PEERS):
        there = slot_of(k, f)
        remote(tgt_out, t1.at[there], sem_t1s.at[i], sem_t1.at[there], partner).wait_recv()
        tsum = tsum + t1[there]
    tsum_out[...] = tsum
    for k in far_first:
        remote(tsum_out.at[k // 2], t2.at[z], sem_t2s.at[k], sem_t2.at[z], at_z(k)).start()
    for n in (2, 3):
        fill_probs(logits2, n, held_blocks[n], n, scale2, other_row)
    sums[2 * BLK:, :] += dot(probs[2 * BLK:, :], tokens2[...], ((1,), (0,)))
    put = pltpu.make_async_copy(sums.at[pl.ds(2 * BLK, QROWS)], own_ref, sem_out)
    put.start()

    trade.wait_send()
    tell.wait_send()
    block = tokens.at[pl.ds(0, 240), pl.ds(0, HALF)]
    remote(block, block, sem_z_send, sem_z.at[0], partner).wait_send()
    whole = chunk_of(tokens, 0)
    for j in range(3):
        remote(whole, whole, sem_x_send.at[j], sem_x.at[j, 0], partner).wait_send()
    for g in range(4):
        remote(whole, whole, sem_c_send.at[g], sem_c.at[g], partner).wait_send()
        remote(whole, whole, sem_y_send.at[g], sem_y.at[g], partner).wait_send()
        remote(whole, whole, sem_c2_send.at[g], sem_c2.at[g], partner).wait_send()
        two = pl.ds(0, 2)
        for i in range(7):
            remote(lse_out.at[two], s1.at[0, two], sem_s1s.at[g, i], sem_s1.at[g, 0], partner).wait_send()
        for k in range(1, NZ):
            remote(l1_out.at[two], s2.at[0, two], sem_s2s.at[g, k], sem_s2.at[g, 0], partner).wait_send()
    for i in range(7):
        remote(tgt_out, t1.at[0], sem_t1s.at[i], sem_t1.at[0], partner).wait_send()
    for k in range(1, NZ):
        remote(tsum_out.at[0], t2.at[0], sem_t2s.at[k], sem_t2.at[0], partner).wait_send()
    tgt = tsum_out[0]
    for k in far_first[::-1]:
        there = lax.rem(z + k, NZ)
        remote(tsum_out.at[0], t2.at[there], sem_t2s.at[k], sem_t2.at[there], partner).wait_recv()
        theirs = t2[there]
        tgt = tgt + (pltpu.roll(theirs, 64, 1) if k % 2 else theirs)
    lane0 = x * 16 + c * 8
    loss = jnp.broadcast_to(l_out[0] - tgt, (8, 128))
    loss_ref[...] = pltpu.roll(loss, lax.rem(128 - lane0, 128), 1)
    put.wait()
    for n in range(2):
        part = recv_ref.at[pl.ds(n * BLK, BLK)]
        remote(send_buf.at[n], part, sem_rs.at[n], sem_rr.at[n], partner).wait()


def body(hidden, embedding, block_counts, lang_blocks, sent_lang, targets):
    vmem, dma = pltpu.VMEM, pltpu.SemaphoreType.DMA
    anywhere = pl.BlockSpec(memory_space=pl.ANY)
    loss, own, received = pl.pallas_call(
        kernel,
        out_shape=(
            jax.ShapeDtypeStruct((8, 128), F32),
            jax.ShapeDtypeStruct((QROWS, D), F32),
            jax.ShapeDtypeStruct((QROWS, D), BF16),
        ),
        in_specs=[anywhere] * 6,
        out_specs=(pl.BlockSpec(memory_space=pltpu.VMEM), anywhere, anywhere),
        scratch_shapes=[
            vmem(hidden.shape, BF16),
            vmem((ROWS, D), BF16),
            vmem((4 * BLK, D), BF16),
            vmem((1, NB), I32),
            vmem(lang_blocks.shape[::-1], I32),
            vmem((1, 64), I32),
            vmem((32, 128), I32),
            vmem((TOK, D), BF16),
            vmem((TOK, D), BF16),
            vmem((ROWS, TOK), F32),
            vmem((4 * BLK, TOK), F32),
            vmem((4 * BLK, TOK), BF16),
            vmem((4 * BLK, D), F32),
            vmem((2, 8, HALF), F32),
            vmem((NB, TOK), F32),
            vmem((8, TOK), I32),
            vmem((8, 8, 1, 128), F32),
            vmem((NZ, 8, 1, 128), F32),
            vmem((8, 8, 1, 128), F32),
            vmem((NZ, 1, 128), F32),
            vmem((8, 1, 128), F32),
            vmem((8, 1, 128), F32),
            vmem((8, 1, 128), F32),
            vmem((8, 1, 128), F32),
            vmem((8, 1, 128), F32),
            vmem((8, 1, 128), F32),
            vmem((2, BLK, D), BF16),
            dma((6,)), dma((2,)), dma, dma((NZ,)), dma((3,)), dma((3, NZ)),
            dma((4,)), dma((4,)), dma((4,)), dma((4,)), dma((4,)), dma((4,)),
            dma((4, 7)), dma((4, 8)), dma((4, NZ)), dma((4, NZ)),
            dma((7,)), dma((8,)), dma((NZ,)), dma((NZ,)),
            dma((2,)), dma((2,)), dma((2,)), dma,
        ],
        compiler_params=pltpu.CompilerParams(
            collective_id=0, has_side_effects=True, vmem_limit_bytes=54 << 20
        ),
    )(
        hidden, embedding, block_counts.reshape(1, NB), lang_blocks.T,
        sent_lang.reshape(1, 64), targets.reshape(32, 128),
    )
    return loss[0, :8], (own + received.astype(F32)).astype(BF16)


def solution(mesh):
    in_specs = (P(("vocab", "batch"), None), P("vocab", None), P("vocab"), P(), P(), P())
    out_specs = (P(("vocab", "batch")), P(("vocab", "batch"), None))
    return jax.shard_map(body, mesh=mesh, in_specs=in_specs, out_specs=out_specs, check_vma=False)
```
